256 devices in a mesh: inner: 16 (over z, y_hi), outer: 4 (over y_lo, core), heads: 4 (over x).
Axes of the slice: x: 4, y: 4 (y_hi: 2, y_lo: 2; y = y_hi * 2 + y_lo), z: 8, core: 2. Of those that a mesh axis runs over, the one named last changes fastest.
Arguments:
- query_states: bfloat16 [8192, 4096], P(('inner', 'outer'), 'heads'), parts along dimension 1, may hold values from -8 to 8
- key_states: bfloat16 [8192, 512], P(('inner', 'outer'), 'heads'), parts along dimension 1, may hold values from -4 to 4
- value_states: bfloat16 [8192, 512], P(('inner', 'outer'), 'heads'), parts along dimension 1, may hold values from -6 to 6
- output_grad: bfloat16 [8192, 4096], P(('inner', 'outer'), 'heads'), parts along dimension 1, may hold values from -2 to 2
- positions: int32 [8192], P(('inner', 'outer')), may hold values from 0 to 8191, as said below
Outputs:
- query_grad: bfloat16 [8192, 4096], P(('inner', 'outer'), 'heads'), parts along dimension 1
- key_grad: bfloat16 [8192, 512], P(('inner', 'outer'), 'heads'), parts along dimension 1
- value_grad: bfloat16 [8192, 512], P(('inner', 'outer'), 'heads'), parts along dimension 1
The draws below stay inside these ranges and needn't reach their ends.
There are 4 independent parts, one for each index of `heads`. The reference program is written for one: setup_inputs(seed, part) draws one part's arguments, and reference() takes and returns one part's arrays. A program takes and returns all parts, laid end to end along the dimension named above; an argument that names none is the same for every part. Nothing has to cross between parts.
Inputs may be any that keep to these rules, and one draw needn't show every extreme that they name: Over all rows every position occurs once; each aligned block of 64 stored rows holds 64 consecutive positions in increasing order, the blocks in an order drawn from the seed.
All inputs are finite; a program needn't handle non-finite values.
Results may differ from the reference program's by a relative error of at most 0.017.
Values may be sent and summed in bfloat16 or wider, within the bound.
No kernel may reach another device: no remote copies, remote signals or barrier semaphores. Data moves between devices by JAX's collectives and lax.ppermute only.
A program may use at most 128 MiB of HBM per device.

```python
import jax
import jax.numpy as jnp
from jax import lax

HD = 128
HQ = 8
TOK_DEV = 128
SPAN = 64
TOKENS = 8192


def shared_keys(key):
    base_key = jax.random.fold_in(key, 11)
    entries = jnp.clip(jax.random.normal(base_key, (TOKENS, HD), jnp.float32), -4.0, 4.0)
    return entries


def draw_key_states(key, part):
    return shared_keys(key).astype(jnp.bfloat16)


def draw_query_states(key, part):
    key = jax.random.fold_in(key, 5)
    entries = jnp.clip(jax.random.normal(key, (TOKENS, HQ, HD), jnp.float32), -4.0, 4.0)
    return entries.reshape(TOKENS, HQ * HD).astype(jnp.bfloat16)


def draw_positions(key, part):
    key = jax.random.fold_in(key, 7)
    span_order = jax.random.permutation(key, TOKENS // SPAN).astype(jnp.int32)
    inside = jnp.arange(SPAN, dtype=jnp.int32)
    return (span_order[:, None] * SPAN + inside[None, :]).reshape(TOKENS)


def levels(key, dims, split, low, top_value):
    factor_of, own = 1.0, jax.random.fold_in(key, 6)
    for dim, parts in split:
        heights = jnp.exp(jax.random.uniform(jax.random.fold_in(own, dim), (parts,), jnp.float32, low / len(split), top_value / len(split)))
        factor_of = factor_of * jnp.repeat(heights, dims[dim] // parts).reshape([-1 if axis == dim else 1 for axis in range(len(dims))])
    return factor_of


def noise(stream_key, extent, spread, bound, cuts=(), kind=jnp.bfloat16):
    values = jax.random.normal(stream_key, extent, jnp.float32) * spread
    if len(cuts) > 0:
        values = levels(stream_key, extent, cuts, -0.22, 0.18) * values
    return jnp.clip(values, min=-bound, max=bound).astype(kind)


def setup_inputs(seed: int = 0, part: int = 0) -> dict:
    seeds = jax.random.split(jax.random.key(seed), 6)
    part_splits = jax.random.split(jax.random.fold_in(seeds[5], part), 6)
    query_states = draw_query_states(jax.random.fold_in(jax.random.fold_in(seeds[5], part), 71), part)
    key_states = draw_key_states(jax.random.fold_in(jax.random.fold_in(seeds[5], part), 71), part)
    value_states = noise(part_splits[2], (TOKENS, HD), 1.0, 6.0, ((0, 64),))
    output_grad = noise(part_splits[3], (TOKENS, HQ * HD), 0.3, 2.0, ((0, 64),))
    positions = draw_positions(jax.random.fold_in(seeds[5], 71), part)
    return {"query_states": query_states, "key_states": key_states, "value_states": value_states, "output_grad": output_grad, "positions": positions}


def contract_last(left, right):
    return lax.dot_general(left, right, (((1,), (1,)), ((), ())), preferred_element_type=jnp.float32)


def contract_first(left, right):
    return lax.dot_general(left, right, (((0,), (0,)), ((), ())), preferred_element_type=jnp.float32)


def reference(query_states, key_states, value_states, output_grad, positions):
    score_scale = HD ** -0.5
    block_count = TOKENS // TOK_DEV
    query_blocks = query_states.reshape(block_count, TOK_DEV * HQ, HD)
    grad_blocks = output_grad.reshape(block_count, TOK_DEV * HQ, HD)
    pos_blocks = jnp.repeat(positions, HQ).reshape(block_count, TOK_DEV * HQ)

    def forward(inputs):
        query_rows, query_pos = inputs
        scores = contract_last(query_rows, key_states) * score_scale
        allowed = positions[None, :] <= query_pos[:, None]
        row_peak = jnp.max(jnp.where(allowed, scores, -jnp.inf), axis=1)
        weights = jnp.where(allowed, jnp.exp(scores - row_peak[:, None]), 0.0)
        row_total = jnp.sum(weights, axis=1)
        attn_sum = jnp.dot(weights.astype(jnp.bfloat16), value_states, preferred_element_type=jnp.float32)
        attn_out = (attn_sum / row_total[:, None]).astype(jnp.bfloat16)
        return attn_out, row_peak + jnp.log(row_total)

    attn_blocks, log_sums = lax.map(forward, (query_blocks, pos_blocks))
    attn_blocks = lax.optimization_barrier(attn_blocks)
    delta_blocks = jnp.sum(grad_blocks.astype(jnp.float32) * attn_blocks.astype(jnp.float32), axis=2)

    def backward(pair_grads, inputs):
        query_rows, grad_rows, query_pos, log_rows, delta_rows = inputs
        scores = contract_last(query_rows, key_states) * score_scale
        allowed = positions[None, :] <= query_pos[:, None]
        attn_probs = jnp.where(allowed, jnp.exp(scores - log_rows[:, None]), 0.0)
        grad_probs = contract_last(grad_rows, value_states)
        grad_scores = attn_probs * (grad_probs - delta_rows[:, None])
        probs_low = attn_probs.astype(jnp.bfloat16)
        scores_low = grad_scores.astype(jnp.bfloat16)
        key_part = contract_first(scores_low, query_rows) * score_scale
        value_part = contract_first(probs_low, grad_rows)
        pair_grads = pair_grads + jnp.concatenate([key_part, value_part], axis=1)
        query_part = jnp.dot(scores_low, key_states, preferred_element_type=jnp.float32) * score_scale
        return pair_grads, query_part.astype(jnp.bfloat16)

    start_grads = jnp.zeros((TOKENS, 2 * HD), jnp.float32)
    pair_grads, query_parts = lax.scan(backward, start_grads, (query_blocks, grad_blocks, pos_blocks, log_sums, delta_blocks))
    query_grad = query_parts.reshape(TOKENS, HQ * HD)
    key_grad = pair_grads[:, :HD].astype(jnp.bfloat16)
    value_grad = pair_grads[:, HD:].astype(jnp.bfloat16)
    return query_grad, key_grad, value_grad
```

```python
import functools

import jax
import jax.numpy as jnp
from jax import lax
from jax.experimental import pallas as pl
from jax.experimental.pallas import tpu as pltpu
from jax.sharding import PartitionSpec as P

F32 = jnp.float32
BF16 = jnp.bfloat16
AXES = ("inner", "outer")
HD = 128
HQ = 8
SPAN = 64
TOK = 128
SHARD = TOK + 16
NZ, NY, NC = 8, 4, 2
ROWS = SPAN * HQ
QB = 2 * NY
KB = 2 * NZ * NC
KEYS = KB * SPAN
CH = 256
SCALE = HD ** -0.5
SCALE2 = SCALE * 1.4426950408889634
NEG = -1e30
VMEM_LIMIT = 48 * 1024 * 1024
FROM_BELOW = (2, 0, 3, 1)
FROM_ABOVE = (1, 3, 0, 2)
FROM_FAR = (3, 2, 1, 0)


def flat(z, y, c):
    return ((z % NZ) * NY + y % NY) * NC + c


def moves(fn):
    return [
        (flat(z, y, c), flat(*fn(z, y, c)))
        for z in range(NZ)
        for y in range(NY)
        for c in range(NC)
    ]


def send(x, fn):
    return lax.ppermute(x, AXES, moves(fn))


def to_core(z, y, c):
    return z, y, 1 - c


def along_y(d):
    return lambda z, y, c: (z, y + d, c)


def along_z(d):
    return lambda z, y, c: (z + d if c == 0 else z - d, y, c)


def dot_nt(a, b):
    return lax.dot_general(a, b, (((1,), (1,)), ((), ())), preferred_element_type=F32)


def dot_nn(a, b):
    return lax.dot_general(a, b, (((1,), (0,)), ((), ())), preferred_element_type=F32)


def key_shards(own_ref, a_ref, x_ref):
    for ref, count in ((own_ref, 2), (a_ref, 7), (x_ref, 7)):
        for i in range(count):
            yield ref, i


def sort_keys(meta, refs, ks, vs):
    for s, (ref, i) in enumerate(key_shards(*refs)):
        for b in range(2):
            row = i * SHARD + b * SPAN
            dst = pl.ds(pl.multiple_of(meta[2 * s + b] * SPAN, SPAN), SPAN)
            ks[dst, :] = ref[row:row + SPAN, 0:HD]
            vs[dst, :] = ref[row:row + SPAN, HD:2 * HD]


def fill_rows(parts, out):
    for r, (ref, row) in enumerate(parts):
        for b in range(2):
            for h in range(HQ):
                at = ((r * 2 + b) * HQ + h) * SPAN
                out[at:at + SPAN, :] = ref[row + b * SPAN:row + (b + 1) * SPAN, h * HD:(h + 1) * HD]


def lead():
    u = lax.broadcasted_iota(jnp.int32, (SPAN, ROWS), 0)
    t = lax.broadcasted_iota(jnp.int32, (SPAN, ROWS), 1) % SPAN
    return u - t


def masked(meta, scores, diff, j, qid, fill):
    parts = []
    for b in range(CH // SPAN):
        gap = (qid - meta[KB + j * (CH // SPAN) + b]) * SPAN
        part = scores[b * SPAN:(b + 1) * SPAN, :]
        parts.append(jnp.where(diff <= gap, part, fill))
    return jnp.concatenate(parts, axis=0)


def bounds(meta, qb):
    full = meta[2 * KB + qb]
    every = meta[2 * KB + QB + qb]
    return full, every, meta[2 * KB + 2 * QB + qb]


def forward_kernel(meta, own, ka, kx, q0, g0, qa, qbelow, qc, gc, st, ks, vs, vt, qs, gs, sc, acc):
    sort_keys(meta, (own, ka, kx), ks, vs)
    for j in range(KEYS // HD):
        vt[0:HD, j * HD:(j + 1) * HD] = vs[j * HD:(j + 1) * HD, :].T
    vt[HD:HD + 16, :] = jnp.ones((16, KEYS), BF16)
    fill_rows(((q0, 0), (qa, 0), (qbelow, 0), (qc, 0)), qs)
    fill_rows(((g0, 0), (qa, SHARD), (qbelow, SHARD), (gc, 0)), gs)

    def block(qb, _):
        rows = pl.ds(pl.multiple_of(qb * ROWS, ROWS), ROWS)
        q = qs[rows, :]
        full, every, qid = bounds(meta, qb)
        diff = lead()

        def score(j, top, mask):
            at = pl.ds(pl.multiple_of(j * CH, CH), CH)
            s = dot_nt(ks[at, :], q) * SCALE2
            if mask:
                s = masked(meta, s, diff, j, qid, NEG)
            sc[at, :] = s
            return jnp.maximum(top, jnp.max(s.reshape(CH // 8, 8, ROWS), axis=0))

        top = jnp.full((8, ROWS), NEG, F32)
        top = lax.fori_loop(0, full, lambda j, t: score(j, t, False), top)
        top = lax.fori_loop(full, every, lambda j, t: score(j, t, True), top)
        peak = jnp.max(top, axis=0, keepdims=True)
        acc[...] = jnp.zeros_like(acc)

        def weigh(j, _):
            at = pl.ds(pl.multiple_of(j * CH, CH), CH)
            e = jnp.exp2(sc[at, :] - peak).astype(BF16)
            acc[...] += dot_nn(vt[:, at], e)
            return 0

        lax.fori_loop(0, every, weigh, 0)
        seen = peak > 0.5 * NEG
        gt = gs[rows, :].T.astype(F32)
        total = jnp.where(seen, acc[HD:HD + 1, :], 0.0)
        dots = jnp.where(seen, jnp.sum(gt * acc[0:HD, :], axis=0, keepdims=True), 0.0)
        at = pl.ds(qb, 1)
        st[0, at, :] = peak
        st[1, at, :] = total
        st[2, at, :] = dots
        return 0

    lax.fori_loop(0, QB, block, 0)


def regroup(x, order):
    return jnp.concatenate([x[2 * i:2 * i + 2, :] for i in order], axis=0)


def backward_kernel(
    meta, own, ka, kx, q0, g0, qa, qbelow, qc, gc, st0, sta, stb, stc,
    dq, dhere, daway, ks, vs, kt, qs, gs, dk, dv, qacc, lse, dlt,
):
    sort_keys(meta, (own, ka, kx), ks, vs)
    for j in range(KEYS // HD):
        kt[:, j * HD:(j + 1) * HD] = ks[j * HD:(j + 1) * HD, :].T
    fill_rows(((q0, 0), (qa, 0), (qbelow, 0), (qc, 0)), qs)
    fill_rows(((g0, 0), (qa, SHARD), (qbelow, SHARD), (gc, 0)), gs)
    same = (0, 1, 2, 3)
    sources = ((st0, same), (sta, FROM_BELOW), (stb, FROM_ABOVE), (stc, FROM_FAR))
    peaks = [regroup(s[0], o) for s, o in sources]
    top = functools.reduce(jnp.maximum, peaks)
    shares = [jnp.exp2(p - top) for p in peaks]
    total = sum(w * regroup(s[1], o) for w, (s, o) in zip(shares, sources))
    dots = sum(w * regroup(s[2], o) for w, (s, o) in zip(shares, sources))
    lse[...] = top + jnp.log2(total)
    dlt[...] = dots / total
    dk[...] = jnp.zeros_like(dk)
    dv[...] = jnp.zeros_like(dv)

    def block(qb, _):
        rows = pl.ds(pl.multiple_of(qb * ROWS, ROWS), ROWS)
        q = qs[rows, :]
        g = gs[rows, :]
        full, every, qid = bounds(meta, qb)
        diff = lead()
        row_lse = lse[pl.ds(qb, 1), :]
        row_dlt = dlt[pl.ds(qb, 1), :]
        qacc[...] = jnp.zeros_like(qacc)

        def step(j, mask):
            at = pl.ds(pl.multiple_of(j * CH, CH), CH)
            p = jnp.exp2(dot_nt(ks[at, :], q) * SCALE2 - row_lse)
            if mask:
                p = masked(meta, p, diff, j, qid, 0.0)
            ds = (p * (dot_nt(vs[at, :], g) - row_dlt)).astype(BF16)
            dv[at, :] += dot_nn(p.astype(BF16), g)
            dk[at, :] += dot_nn(ds, q)
            qacc[...] += dot_nn(kt[:, at], ds)
            return 0

        lax.fori_loop(0, full, lambda j, _: step(j, False), 0)
        lax.fori_loop(full, every, lambda j, _: step(j, True), 0)
        done = (qacc[...] * SCALE).T.astype(BF16)
        for h in range(HQ):
            dq[qb // 2, pl.ds(pl.multiple_of((qb % 2) * SPAN, SPAN), SPAN), h * HD:(h + 1) * HD] = (
                done[h * SPAN:(h + 1) * SPAN, :]
            )
        return 0

    lax.fori_loop(0, QB, block, 0)
    for s in range(2 * NZ):
        for b in range(2):
            src = pl.ds(pl.multiple_of(meta[2 * s + b] * SPAN, SPAN), SPAN)
            if s == 0:
                ref, i = dhere, 0
            elif s == 1:
                ref, i = daway, 0
            elif s < 9:
                ref, i = dhere, s - 1
            else:
                ref, i = daway, s - 8
            row = i * TOK + b * SPAN
            ref[row:row + SPAN, 0:HD] = (dk[src, :] * SCALE).astype(BF16)
            ref[row:row + SPAN, HD:2 * HD] = dv[src, :].astype(BF16)


def call(body, outs, scratch, flops):
    vmem = pl.BlockSpec(memory_space=pltpu.VMEM)
    smem = pl.BlockSpec(memory_space=pltpu.SMEM)

    def run(meta, *args):
        return pl.pallas_call(
            body,
            out_shape=outs,
            in_specs=[smem] + [vmem] * len(args),
            out_specs=jax.tree.map(lambda _: vmem, outs),
            scratch_shapes=scratch,
            compiler_params=pltpu.CompilerParams(vmem_limit_bytes=VMEM_LIMIT),
            cost_estimate=pl.CostEstimate(
                flops=flops, bytes_accessed=6 * 1024 * 1024, transcendentals=QB * ROWS * KEYS // 2
            ),
        )(meta, *args)

    return run


def shape(*dims, dtype=BF16):
    return jax.ShapeDtypeStruct(dims, dtype)


def on_device(query_states, key_states, value_states, output_grad, positions):
    own_ids = (positions[::SPAN] // SPAN).astype(BF16)
    kv = jnp.concatenate(
        [
            jnp.concatenate([key_states, value_states], axis=1),
            jnp.broadcast_to(jnp.repeat(own_ids, HD)[None, :], (16, 2 * HD)),
        ],
        axis=0,
    )
    qg = jnp.concatenate(
        [
            query_states,
            jnp.broadcast_to(jnp.repeat(own_ids, 4 * HD)[None, :], (16, HQ * HD)),
            output_grad,
        ],
        axis=0,
    )
    qa = send(qg, along_y(1))
    qb = send(qg, along_y(-1))
    qc = send(qa[:SHARD], along_y(1))
    gc = send(qb[SHARD:], along_y(-1))
    far = send(kv, along_z(4))
    pair = jnp.concatenate([kv, send(kv, to_core)], axis=0)
    near = [send(pair, along_z(d)) for d in (3, 2, 1)]
    ka = jnp.concatenate(near[::-1] + [far], axis=0)
    kx = send(ka, to_core)

    def ids_of(x):
        return x.reshape(-1, SHARD, 2 * HD)[:, TOK, ::HD].reshape(-1)

    kid = jnp.concatenate([ids_of(pair), ids_of(ka), ids_of(kx)]).astype(jnp.int32)
    qid = jnp.concatenate(
        [own_ids] + [x[TOK, :: 4 * HD] for x in (qa, qb, qc)]
    ).astype(jnp.int32)
    rank = jnp.sum((kid[None, :] < kid[:, None]).astype(jnp.int32), axis=1)
    slots = jnp.arange(KB, dtype=jnp.int32)
    in_order = jnp.sum(jnp.where(rank[None, :] == slots[:, None], kid[None, :], 0), axis=1)
    below = jnp.sum((kid[None, :] < qid[:, None]).astype(jnp.int32), axis=1)
    upto = jnp.sum((kid[None, :] <= qid[:, None]).astype(jnp.int32), axis=1)
    per = CH // SPAN
    meta = jnp.concatenate([rank, in_order, below // per, (upto + per - 1) // per, qid])

    rows = QB * ROWS
    args = (pair, ka, kx, query_states, output_grad, qa, qb, qc, gc)
    kv_scratch = [pltpu.VMEM((KEYS, HD), BF16), pltpu.VMEM((KEYS, HD), BF16)]
    q_scratch = [pltpu.VMEM((rows, HD), BF16), pltpu.VMEM((rows, HD), BF16)]
    st = call(
        forward_kernel,
        shape(3, QB, ROWS, dtype=F32),
        kv_scratch
        + [pltpu.VMEM((HD + 16, KEYS), BF16)]
        + q_scratch
        + [pltpu.VMEM((KEYS, ROWS), F32), pltpu.VMEM((HD + 16, ROWS), F32)],
        2 * rows * KEYS * HD,
    )(meta, *args)
    stats = (st, send(st, along_y(1)), send(st, along_y(-1)), send(st, along_y(2)))
    dq, here, away = call(
        backward_kernel,
        (shape(NY, TOK, HQ * HD), shape(8 * TOK, 2 * HD), shape(8 * TOK, 2 * HD)),
        kv_scratch
        + [pltpu.VMEM((HD, KEYS), BF16)]
        + q_scratch
        + [pltpu.VMEM((KEYS, HD), F32), pltpu.VMEM((KEYS, HD), F32), pltpu.VMEM((HD, ROWS), F32)]
        + [pltpu.VMEM((QB, ROWS), F32), pltpu.VMEM((QB, ROWS), F32)],
        5 * rows * KEYS * HD,
    )(meta, *args, *stats)

    terms = [dq[0], send(dq[3], along_y(2)), send(dq[1], along_y(-1)), send(dq[2], along_y(1))]
    query_grad = sum(t.astype(F32) for t in terms).astype(BF16)
    both = here.astype(F32) + send(away, to_core).astype(F32)
    out = both[TOK:].astype(BF16)
    back = [send(out[(2 * d - 2) * TOK:2 * d * TOK], along_z(-d)) for d in (3, 2, 1)]
    back_far = send(out[6 * TOK:], along_z(-4))
    found = sum(t.astype(F32) for t in back)
    cross = send(found[TOK:].astype(BF16), to_core)
    pair_grad = both[:TOK] + back_far.astype(F32) + found[:TOK] + cross.astype(F32)
    return (
        query_grad,
        pair_grad[:, :HD].astype(BF16),
        pair_grad[:, HD:].astype(BF16),
    )


def solution(mesh):
    in_specs = (
        P(("inner", "outer"), "heads"),
        P(("inner", "outer"), "heads"),
        P(("inner", "outer"), "heads"),
        P(("inner", "outer"), "heads"),
        P(("inner", "outer")),
    )
    out_specs = (
        P(("inner", "outer"), "heads"),
        P(("inner", "outer"), "heads"),
        P(("inner", "outer"), "heads"),
    )
    return jax.shard_map(
        on_device, mesh=mesh, in_specs=in_specs, out_specs=out_specs, check_vma=False
    )
```

```python
import functools

import jax
import jax.numpy as jnp
from jax import lax
from jax.experimental import pallas as pl
from jax.experimental.pallas import tpu as pltpu
from jax.sharding import PartitionSpec as P

F32 = jnp.float32
BF16 = jnp.bfloat16
AXES = ("inner", "outer")
HD = 128
HQ = 8
SPAN = 64
TOK = 128
SHARD = TOK + 16
NZ, NY, NC = 8, 4, 2
ROWS = SPAN * HQ
QB = 2 * NY
KB = 2 * NZ * NC
KEYS = KB * SPAN
CH = 512
SCALE = HD ** -0.5
SCALE2 = SCALE * 1.4426950408889634
NEG = -1e30
VMEM_LIMIT = 48 * 1024 * 1024
FROM_BELOW = (2, 0, 3, 1)
FROM_ABOVE = (1, 3, 0, 2)
FROM_FAR = (3, 2, 1, 0)


def flat(z, y, c):
    return ((z % NZ) * NY + y % NY) * NC + c


def moves(fn):
    return [
        (flat(z, y, c), flat(*fn(z, y, c)))
        for z in range(NZ)
        for y in range(NY)
        for c in range(NC)
    ]


def send(x, fn):
    return lax.ppermute(x, AXES, moves(fn))


def to_core(z, y, c):
    return z, y, 1 - c


def along_y(d):
    return lambda z, y, c: (z, y + d, c)


def along_z(d):
    return lambda z, y, c: (z + d if c == 0 else z - d, y, c)


def dot_nt(a, b):
    return lax.dot_general(a, b, (((1,), (1,)), ((), ())), preferred_element_type=F32)


def dot_nn(a, b):
    return lax.dot_general(a, b, (((1,), (0,)), ((), ())), preferred_element_type=F32)


def key_shards(own_ref, a_ref, x_ref):
    for ref, count in ((own_ref, 2), (a_ref, 7), (x_ref, 7)):
        for i in range(count):
            yield ref, i


def sort_keys(meta, refs, ks, vs):
    for s, (ref, i) in enumerate(key_shards(*refs)):
        for b in range(2):
            row = i * SHARD + b * SPAN
            dst = pl.ds(pl.multiple_of(meta[2 * s + b] * SPAN, SPAN), SPAN)
            ks[dst, :] = ref[row:row + SPAN, 0:HD]
            vs[dst, :] = ref[row:row + SPAN, HD:2 * HD]


def fill_rows(parts, out):
    for r, (ref, row) in enumerate(parts):
        for b in range(2):
            for h in range(HQ):
                at = ((r * 2 + b) * HQ + h) * SPAN
                out[at:at + SPAN, :] = ref[row + b * SPAN:row + (b + 1) * SPAN, h * HD:(h + 1) * HD]


def lead():
    u = lax.broadcasted_iota(jnp.int32, (SPAN, ROWS), 0)
    t = lax.broadcasted_iota(jnp.int32, (SPAN, ROWS), 1) % SPAN
    return u - t


def tasks_of(meta, info):
    def idle(t):
        info[0, t] = 0
        info[1, t] = 0
        info[2, t] = -1

    idle(0)
    idle(1)

    def block(qb, t):
        chunks = meta[2 * KB + qb]
        qid = meta[2 * KB + QB + qb]

        def put(j, _):
            info[0, t + j] = qb
            info[1, t + j] = j
            info[2, t + j] = qid
            return 0

        lax.fori_loop(0, chunks, put, 0)
        return t + chunks

    end = lax.fori_loop(0, QB, block, 2)
    idle(end)
    idle(end + 1)
    return end + 2


def masked(meta, scores, diff, j, qid, fill):
    parts = []
    for b in range(CH // SPAN):
        gap = (qid - meta[KB + j * (CH // SPAN) + b]) * SPAN
        part = scores[b * SPAN:(b + 1) * SPAN, :]
        parts.append(jnp.where(diff <= gap, part, fill))
    return jnp.concatenate(parts, axis=0)


def query_rows(qb):
    return pl.ds(pl.multiple_of(qb * ROWS, ROWS), ROWS)


def key_rows(j):
    return pl.ds(pl.multiple_of(j * CH, CH), CH)


def forward_kernel(
    meta, own, ka, kx, q0, g0, qa, qbelow, qc, gc, st,
    ks, vs, vt, qs, gs, gt, info, sc, ex, mx, hi,
):
    sort_keys(meta, (own, ka, kx), ks, vs)
    for j in range(KEYS // HD):
        vt[0:HD, j * HD:(j + 1) * HD] = vs[j * HD:(j + 1) * HD, :].T
    vt[HD:HD + 16, :] = jnp.ones((16, KEYS), BF16)
    fill_rows(((q0, 0), (qa, 0), (qbelow, 0), (qc, 0)), qs)
    fill_rows(((g0, 0), (qa, SHARD), (qbelow, SHARD), (gc, 0)), gs)
    for j in range(QB):
        gt[j, :, :] = gs[j * ROWS:(j + 1) * ROWS, :].T
    end = tasks_of(meta, info)
    st[0, :, :] = jnp.full((QB, ROWS), NEG, F32)
    st[1, :, :] = jnp.zeros((QB, ROWS), F32)
    st[2, :, :] = jnp.zeros((QB, ROWS), F32)
    sc[...] = jnp.full_like(sc, NEG)
    ex[...] = jnp.zeros_like(ex)
    mx[...] = jnp.full_like(mx, NEG)
    hi[...] = jnp.full_like(hi, NEG)
    diff = lead()

    def step(t, _):
        qb = info[0, t - 2]
        acc = dot_nn(vt[:, key_rows(info[1, t - 2])], ex[...])
        total = acc[HD:HD + 1, :]
        dots = jnp.sum(gt[qb].astype(F32) * acc[0:HD, :], axis=0, keepdims=True)
        at = pl.ds(qb, 1)
        peak, old = mx[...], st[0, at, :]
        top = jnp.maximum(peak, old)
        new_w, old_w = jnp.exp2(peak - top), jnp.exp2(old - top)
        st[0, at, :] = top
        st[1, at, :] = st[1, at, :] * old_w + total * new_w
        st[2, at, :] = st[2, at, :] * old_w + dots * new_w
        peak = jnp.max(hi[...], axis=0, keepdims=True)
        mx[...] = peak
        ex[...] = jnp.exp2(sc[...] - peak).astype(BF16)
        s = dot_nt(ks[key_rows(info[1, t]), :], qs[query_rows(info[0, t]), :]) * SCALE2
        s = masked(meta, s, diff, info[1, t], info[2, t], NEG)
        sc[...] = s
        hi[...] = jnp.max(s.reshape(CH // 8, 8, ROWS), axis=0)
        return 0

    lax.fori_loop(2, end, step, 0)


def regroup(x, order):
    return jnp.concatenate([x[2 * i:2 * i + 2, :] for i in order], axis=0)


def backward_kernel(
    meta, own, ka, kx, q0, g0, qa, qbelow, qc, gc, st0, sta, stb, stc,
    dq, dhere, daway, ks, vs, kt, qs, gs, dk, dv, qacc, lse, dlt, info, pb, db,
):
    sort_keys(meta, (own, ka, kx), ks, vs)
    for j in range(KEYS // HD):
        kt[:, j * HD:(j + 1) * HD] = ks[j * HD:(j + 1) * HD, :].T
    fill_rows(((q0, 0), (qa, 0), (qbelow, 0), (qc, 0)), qs)
    fill_rows(((g0, 0), (qa, SHARD), (qbelow, SHARD), (gc, 0)), gs)
    same = (0, 1, 2, 3)
    sources = ((st0, same), (sta, FROM_BELOW), (stb, FROM_ABOVE), (stc, FROM_FAR))
    peaks = [regroup(s[0], o) for s, o in sources]
    top = functools.reduce(jnp.maximum, peaks)
    shares = [jnp.exp2(p - top) for p in peaks]
    total = sum(w * regroup(s[1], o) for w, (s, o) in zip(shares, sources))
    dots = sum(w * regroup(s[2], o) for w, (s, o) in zip(shares, sources))
    lse[...] = top + jnp.log2(total)
    dlt[...] = dots / total
    for ref in (dk, dv, qacc, pb, db):
        ref[...] = jnp.zeros_like(ref)
    end = tasks_of(meta, info)
    diff = lead()

    def step(t, _):
        qb, at = info[0, t - 1], key_rows(info[1, t - 1])
        rows = query_rows(qb)
        p, ds = pb[...], db[...]
        dv[at, :] += dot_nn(p, gs[rows, :])
        dk[at, :] += dot_nn(ds, qs[rows, :])
        qacc[qb] += dot_nn(kt[:, at], ds)
        qb = info[0, t]
        rows, at = query_rows(qb), key_rows(info[1, t])
        s = dot_nt(ks[at, :], qs[rows, :]) * SCALE2
        p = jnp.exp2(s - lse[pl.ds(qb, 1), :])
        p = masked(meta, p, diff, info[1, t], info[2, t], 0.0)
        pb[...] = p.astype(BF16)
        db[...] = (p * (dot_nt(vs[at, :], gs[rows, :]) - dlt[pl.ds(qb, 1), :])).astype(BF16)
        return 0

    lax.fori_loop(2, end, step, 0)
    for i in range(QB):
        done = (qacc[i] * SCALE).T.astype(BF16)
        for h in range(HQ):
            row = (i % 2) * SPAN
            dq[i // 2, row:row + SPAN, h * HD:(h + 1) * HD] = done[h * SPAN:(h + 1) * SPAN, :]
    for s in range(2 * NZ):
        for b in range(2):
            src = pl.ds(pl.multiple_of(meta[2 * s + b] * SPAN, SPAN), SPAN)
            if s == 0:
                ref, i = dhere, 0
            elif s == 1:
                ref, i = daway, 0
            elif s < 9:
                ref, i = dhere, s - 1
            else:
                ref, i = daway, s - 8
            row = i * TOK + b * SPAN
            ref[row:row + SPAN, 0:HD] = (dk[src, :] * SCALE).astype(BF16)
            ref[row:row + SPAN, HD:2 * HD] = dv[src, :].astype(BF16)


def call(body, outs, scratch, flops):
    vmem = pl.BlockSpec(memory_space=pltpu.VMEM)
    smem = pl.BlockSpec(memory_space=pltpu.SMEM)

    def run(meta, *args):
        return pl.pallas_call(
            body,
            out_shape=outs,
            in_specs=[smem] + [vmem] * len(args),
            out_specs=jax.tree.map(lambda _: vmem, outs),
            scratch_shapes=scratch,
            compiler_params=pltpu.CompilerParams(vmem_limit_bytes=VMEM_LIMIT),
            cost_estimate=pl.CostEstimate(
                flops=flops, bytes_accessed=6 * 1024 * 1024, transcendentals=QB * ROWS * KEYS // 2
            ),
        )(meta, *args)

    return run


def shape(*dims, dtype=BF16):
    return jax.ShapeDtypeStruct(dims, dtype)


INFO = pltpu.SMEM((3, QB * KEYS // CH + 4), jnp.int32)


def fwd_call(meta, *args):
    rows = QB * ROWS
    return call(
        forward_kernel,
        shape(3, QB, ROWS, dtype=F32),
        [
            pltpu.VMEM((KEYS, HD), BF16),
            pltpu.VMEM((KEYS, HD), BF16),
            pltpu.VMEM((HD + 16, KEYS), BF16),
            pltpu.VMEM((rows, HD), BF16),
            pltpu.VMEM((rows, HD), BF16),
            pltpu.VMEM((QB, HD, ROWS), BF16),
            INFO,
            pltpu.VMEM((CH, ROWS), F32),
            pltpu.VMEM((CH, ROWS), BF16),
            pltpu.VMEM((1, ROWS), F32),
            pltpu.VMEM((8, ROWS), F32),
        ],
        2 * rows * KEYS * HD,
    )(meta, *args)


def bwd_call(meta, *args):
    rows = QB * ROWS
    return call(
        backward_kernel,
        (shape(NY, TOK, HQ * HD), shape(8 * TOK, 2 * HD), shape(8 * TOK, 2 * HD)),
        [
            pltpu.VMEM((KEYS, HD), BF16),
            pltpu.VMEM((KEYS, HD), BF16),
            pltpu.VMEM((HD, KEYS), BF16),
            pltpu.VMEM((rows, HD), BF16),
            pltpu.VMEM((rows, HD), BF16),
            pltpu.VMEM((KEYS, HD), F32),
            pltpu.VMEM((KEYS, HD), F32),
            pltpu.VMEM((QB, HD, ROWS), F32),
            pltpu.VMEM((QB, ROWS), F32),
            pltpu.VMEM((QB, ROWS), F32),
            INFO,
            pltpu.VMEM((CH, ROWS), BF16),
            pltpu.VMEM((CH, ROWS), BF16),
        ],
        5 * rows * KEYS * HD,
    )(meta, *args)


def on_device(query_states, key_states, value_states, output_grad, positions):
    own_ids = (positions[::SPAN] // SPAN).astype(BF16)
    kv = jnp.concatenate(
        [
            jnp.concatenate([key_states, value_states], axis=1),
            jnp.broadcast_to(jnp.repeat(own_ids, HD)[None, :], (16, 2 * HD)),
        ],
        axis=0,
    )
    qg = jnp.concatenate(
        [
            query_states,
            jnp.broadcast_to(jnp.repeat(own_ids, 4 * HD)[None, :], (16, HQ * HD)),
            output_grad,
        ],
        axis=0,
    )
    qg, kv = lax.optimization_barrier((qg, kv))
    qa = send(qg, along_y(1))
    qb = send(qg, along_y(-1))
    pair = jnp.concatenate([kv, send(kv, to_core)], axis=0)
    second = send(pair, along_z(2))
    first = send(pair, along_z(1))
    first, second, qa, qb = lax.optimization_barrier((first, second, qa, qb))
    qc = send(qa[:SHARD], along_y(1))
    gc = send(qb[SHARD:], along_y(-1))
    far = send(second[:SHARD], along_z(2))
    third = send(second, along_z(1))
    ka = jnp.concatenate([first, second, third, far], axis=0)
    kx = send(ka, to_core)

    def ids_of(x):
        return x.reshape(-1, SHARD, 2 * HD)[:, TOK, ::HD].reshape(-1)

    kid = jnp.concatenate([ids_of(pair), ids_of(ka), ids_of(kx)]).astype(jnp.int32)
    qid = jnp.concatenate(
        [own_ids] + [x[TOK, :: 4 * HD] for x in (qa, qb, qc)]
    ).astype(jnp.int32)
    rank = jnp.sum((kid[None, :] < kid[:, None]).astype(jnp.int32), axis=1)
    slots = jnp.arange(KB, dtype=jnp.int32)
    in_order = jnp.sum(jnp.where(rank[None, :] == slots[:, None], kid[None, :], 0), axis=1)
    upto = jnp.sum((kid[None, :] <= qid[:, None]).astype(jnp.int32), axis=1)
    per = CH // SPAN
    meta = jnp.concatenate([rank, in_order, (upto + per - 1) // per, qid])

    args = (pair, ka, kx, query_states, output_grad, qa, qb, qc, gc)
    st = fwd_call(meta, *args)
    stats = (st, send(st, along_y(1)), send(st, along_y(-1)), send(st, along_y(2)))
    dq, here, away = bwd_call(meta, *args, *stats)

    terms = [dq[0], send(dq[3], along_y(2)), send(dq[1], along_y(-1)), send(dq[2], along_y(1))]
    query_grad = sum(t.astype(F32) for t in terms).astype(BF16)
    both = here.astype(F32) + send(away, to_core).astype(F32)
    out = both[TOK:].astype(BF16)
    back = [send(out[(2 * d - 2) * TOK:2 * d * TOK], along_z(-d)) for d in (3, 2, 1)]
    back_far = send(out[6 * TOK:], along_z(-4))
    found = sum(t.astype(F32) for t in back)
    cross = send(found[TOK:].astype(BF16), to_core)
    pair_grad = both[:TOK] + back_far.astype(F32) + found[:TOK] + cross.astype(F32)
    return (
        query_grad,
        pair_grad[:, :HD].astype(BF16),
        pair_grad[:, HD:].astype(BF16),
    )


def solution(mesh):
    in_specs = (
        P(("inner", "outer"), "heads"),
        P(("inner", "outer"), "heads"),
        P(("inner", "outer"), "heads"),
        P(("inner", "outer"), "heads"),
        P(("inner", "outer")),
    )
    out_specs = (
        P(("inner", "outer"), "heads"),
        P(("inner", "outer"), "heads"),
        P(("inner", "outer"), "heads"),
    )
    return jax.shard_map(
        on_device, mesh=mesh, in_specs=in_specs, out_specs=out_specs, check_vma=False
    )
```

```python
import functools

import jax
import jax.numpy as jnp
from jax import lax
from jax.experimental import pallas as pl
from jax.experimental.pallas import tpu as pltpu
from jax.sharding import PartitionSpec as P

F32 = jnp.float32
BF16 = jnp.bfloat16
AXES = ("inner", "outer")
HD = 128
HQ = 8
SPAN = 64
TOK = 128
SHARD = TOK + 16
NZ, NY, NC = 8, 4, 2
ROWS = SPAN * HQ
QB = 2 * NY
KB = 2 * NZ * NC
KEYS = KB * SPAN
CH = 512
SCALE = HD ** -0.5
SCALE2 = SCALE * 1.4426950408889634
NEG = -1e30
VMEM_LIMIT = 48 * 1024 * 1024
FROM_BELOW = (2, 0, 3, 1)
FROM_ABOVE = (1, 3, 0, 2)
FROM_FAR = (3, 2, 1, 0)


def flat(z, y, c):
    return ((z % NZ) * NY + y % NY) * NC + c


def moves(fn):
    return [
        (flat(z, y, c), flat(*fn(z, y, c)))
        for z in range(NZ)
        for y in range(NY)
        for c in range(NC)
    ]


def send(x, fn):
    return lax.ppermute(x, AXES, moves(fn))


def to_core(z, y, c):
    return z, y, 1 - c


def along_y(d):
    return lambda z, y, c: (z, y + d, c)


def along_z(d):
    return lambda z, y, c: (z + d if c == 0 else z - d, y, c)


def dot_nt(a, b):
    return lax.dot_general(a, b, (((1,), (1,)), ((), ())), preferred_element_type=F32)


def dot_nn(a, b):
    return lax.dot_general(a, b, (((1,), (0,)), ((), ())), preferred_element_type=F32)


def key_shards(own_ref, a_ref, x_ref):
    for ref, count in ((own_ref, 2), (a_ref, 7), (x_ref, 7)):
        for i in range(count):
            yield ref, i


def sort_keys(meta, refs, ks, vs):
    for s, (ref, i) in enumerate(key_shards(*refs)):
        for b in range(2):
            row = i * SHARD + b * SPAN
            dst = pl.ds(pl.multiple_of(meta[2 * s + b] * SPAN, SPAN), SPAN)
            ks[dst, :] = ref[row:row + SPAN, 0:HD]
            vs[dst, :] = ref[row:row + SPAN, HD:2 * HD]


def fill_rows(parts, out):
    for r, (ref, row) in enumerate(parts):
        for b in range(2):
            for h in range(HQ):
                at = ((r * 2 + b) * HQ + h) * SPAN
                out[at:at + SPAN, :] = ref[row + b * SPAN:row + (b + 1) * SPAN, h * HD:(h + 1) * HD]


def lead():
    u = lax.broadcasted_iota(jnp.int32, (SPAN, ROWS), 0)
    t = lax.broadcasted_iota(jnp.int32, (SPAN, ROWS), 1) % SPAN
    return u - t


def tasks_of(meta, info):
    def idle(t):
        info[0, t] = 0
        info[1, t] = 0
        info[2, t] = -1

    idle(0)
    idle(1)

    def block(qb, t):
        chunks = meta[2 * KB + qb]
        qid = meta[2 * KB + QB + qb]

        def put(j, _):
            info[0, t + j] = qb
            info[1, t + j] = j
            info[2, t + j] = qid
            return 0

        lax.fori_loop(0, chunks, put, 0)
        return t + chunks

    end = lax.fori_loop(0, QB, block, 2)
    idle(end)
    idle(end + 1)
    return end + 2


def masked(meta, scores, diff, j, qid, fill):
    parts = []
    for b in range(CH // SPAN):
        gap = (qid - meta[KB + j * (CH // SPAN) + b]) * SPAN
        part = scores[b * SPAN:(b + 1) * SPAN, :]
        parts.append(jnp.where(diff <= gap, part, fill))
    return jnp.concatenate(parts, axis=0)


def query_rows(qb):
    return pl.ds(pl.multiple_of(qb * ROWS, ROWS), ROWS)


def key_rows(j):
    return pl.ds(pl.multiple_of(j * CH, CH), CH)


def forward_kernel(
    meta, own, ka, kx, q0, g0, qa, qbelow, qc, gc, st,
    ks, vs, vt, qs, gs, gt, info, sc, ex, mx, hi,
):
    sort_keys(meta, (own, ka, kx), ks, vs)
    for j in range(KEYS // HD):
        vt[0:HD, j * HD:(j + 1) * HD] = vs[j * HD:(j + 1) * HD, :].T
    vt[HD:HD + 16, :] = jnp.ones((16, KEYS), BF16)
    fill_rows(((q0, 0), (qa, 0), (qbelow, 0), (qc, 0)), qs)
    fill_rows(((g0, 0), (qa, SHARD), (qbelow, SHARD), (gc, 0)), gs)
    for j in range(QB):
        gt[j, :, :] = gs[j * ROWS:(j + 1) * ROWS, :].T
    end = tasks_of(meta, info)
    st[0, :, :] = jnp.full((QB, ROWS), NEG, F32)
    st[1, :, :] = jnp.zeros((QB, ROWS), F32)
    st[2, :, :] = jnp.zeros((QB, ROWS), F32)
    sc[...] = jnp.full_like(sc, NEG)
    ex[...] = jnp.zeros_like(ex)
    mx[...] = jnp.full_like(mx, NEG)
    hi[...] = jnp.full_like(hi, NEG)
    diff = lead()

    def step(t, _):
        qb = info[0, t - 2]
        acc = dot_nn(vt[:, key_rows(info[1, t - 2])], ex[...])
        total = acc[HD:HD + 1, :]
        dots = jnp.sum(gt[qb].astype(F32) * acc[0:HD, :], axis=0, keepdims=True)
        at = pl.ds(qb, 1)
        peak, old = mx[...], st[0, at, :]
        top = jnp.maximum(peak, old)
        new_w, old_w = jnp.exp2(peak - top), jnp.exp2(old - top)
        st[0, at, :] = top
        st[1, at, :] = st[1, at, :] * old_w + total * new_w
        st[2, at, :] = st[2, at, :] * old_w + dots * new_w
        peak = jnp.max(hi[...], axis=0, keepdims=True)
        mx[...] = peak
        ex[...] = jnp.exp2(sc[...] - peak).astype(BF16)
        s = dot_nt(ks[key_rows(info[1, t]), :], qs[query_rows(info[0, t]), :]) * SCALE2
        s = masked(meta, s, diff, info[1, t], info[2, t], NEG)
        sc[...] = s
        hi[...] = jnp.max(s.reshape(CH // 8, 8, ROWS), axis=0)
        return 0

    lax.fori_loop(2, end, step, 0)


def regroup(x, order):
    return jnp.concatenate([x[2 * i:2 * i + 2, :] for i in order], axis=0)


def backward_kernel(
    meta, own, ka, kx, q0, g0, qa, qbelow, qc, gc, st0, sta, stb, stc,
    dq, dhere, daway, ks, vs, kt, qs, gs, dk, dv, qacc, lse, dlt, info, pb, db,
):
    sort_keys(meta, (own, ka, kx), ks, vs)
    for j in range(KEYS // HD):
        kt[:, j * HD:(j + 1) * HD] = ks[j * HD:(j + 1) * HD, :].T
    fill_rows(((q0, 0), (qa, 0), (qbelow, 0), (qc, 0)), qs)
    fill_rows(((g0, 0), (qa, SHARD), (qbelow, SHARD), (gc, 0)), gs)
    same = (0, 1, 2, 3)
    sources = ((st0, same), (sta, FROM_BELOW), (stb, FROM_ABOVE), (stc, FROM_FAR))
    peaks = [regroup(s[0], o) for s, o in sources]
    top = functools.reduce(jnp.maximum, peaks)
    shares = [jnp.exp2(p - top) for p in peaks]
    total = sum(w * regroup(s[1], o) for w, (s, o) in zip(shares, sources))
    dots = sum(w * regroup(s[2], o) for w, (s, o) in zip(shares, sources))
    lse[...] = top + jnp.log2(total)
    dlt[...] = dots / total
    for ref in (dk, dv, qacc, pb, db):
        ref[...] = jnp.zeros_like(ref)
    end = tasks_of(meta, info)
    diff = lead()

    def step(t, _):
        qb, at = info[0, t - 1], key_rows(info[1, t - 1])
        rows = query_rows(qb)
        p, ds = pb[...], db[...]
        dv[at, :] += dot_nn(p, gs[rows, :])
        dk[at, :] += dot_nn(ds, qs[rows, :])
        qacc[qb] += dot_nn(kt[:, at], ds)
        qb = info[0, t]
        rows, at = query_rows(qb), key_rows(info[1, t])
        s = dot_nt(ks[at, :], qs[rows, :]) * SCALE2
        p = jnp.exp2(s - lse[pl.ds(qb, 1), :])
        p = masked(meta, p, diff, info[1, t], info[2, t], 0.0)
        pb[...] = p.astype(BF16)
        db[...] = (p * (dot_nt(vs[at, :], gs[rows, :]) - dlt[pl.ds(qb, 1), :])).astype(BF16)
        return 0

    lax.fori_loop(2, end, step, 0)
    for i in range(QB):
        done = (qacc[i] * SCALE).T.astype(BF16)
        for h in range(HQ):
            row = (i % 2) * SPAN
            dq[i // 2, row:row + SPAN, h * HD:(h + 1) * HD] = done[h * SPAN:(h + 1) * SPAN, :]
    for s in range(2 * NZ):
        for b in range(2):
            src = pl.ds(pl.multiple_of(meta[2 * s + b] * SPAN, SPAN), SPAN)
            if s == 0:
                ref, i = dhere, 0
            elif s == 1:
                ref, i = daway, 0
            elif s < 9:
                ref, i = dhere, s - 1
            else:
                ref, i = daway, s - 8
            row = i * TOK + b * SPAN
            ref[row:row + SPAN, 0:HD] = (dk[src, :] * SCALE).astype(BF16)
            ref[row:row + SPAN, HD:2 * HD] = dv[src, :].astype(BF16)


def call(body, outs, scratch, flops):
    vmem = pl.BlockSpec(memory_space=pltpu.VMEM)
    smem = pl.BlockSpec(memory_space=pltpu.SMEM)

    def run(meta, *args):
        return pl.pallas_call(
            body,
            out_shape=outs,
            in_specs=[smem] + [vmem] * len(args),
            out_specs=jax.tree.map(lambda _: vmem, outs),
            scratch_shapes=scratch,
            compiler_params=pltpu.CompilerParams(vmem_limit_bytes=VMEM_LIMIT),
            cost_estimate=pl.CostEstimate(
                flops=flops, bytes_accessed=6 * 1024 * 1024, transcendentals=QB * ROWS * KEYS // 2
            ),
        )(meta, *args)

    return run


def shape(*dims, dtype=BF16):
    return jax.ShapeDtypeStruct(dims, dtype)


INFO = pltpu.SMEM((3, QB * KEYS // CH + 4), jnp.int32)


def fwd_call(meta, *args):
    rows = QB * ROWS
    return call(
        forward_kernel,
        shape(3, QB, ROWS, dtype=F32),
        [
            pltpu.VMEM((KEYS, HD), BF16),
            pltpu.VMEM((KEYS, HD), BF16),
            pltpu.VMEM((HD + 16, KEYS), BF16),
            pltpu.VMEM((rows, HD), BF16),
            pltpu.VMEM((rows, HD), BF16),
            pltpu.VMEM((QB, HD, ROWS), BF16),
            INFO,
            pltpu.VMEM((CH, ROWS), F32),
            pltpu.VMEM((CH, ROWS), BF16),
            pltpu.VMEM((1, ROWS), F32),
            pltpu.VMEM((8, ROWS), F32),
        ],
        2 * rows * KEYS * HD,
    )(meta, *args)


def bwd_call(meta, *args):
    rows = QB * ROWS
    return call(
        backward_kernel,
        (shape(NY, TOK, HQ * HD), shape(8 * TOK, 2 * HD), shape(8 * TOK, 2 * HD)),
        [
            pltpu.VMEM((KEYS, HD), BF16),
            pltpu.VMEM((KEYS, HD), BF16),
            pltpu.VMEM((HD, KEYS), BF16),
            pltpu.VMEM((rows, HD), BF16),
            pltpu.VMEM((rows, HD), BF16),
            pltpu.VMEM((KEYS, HD), F32),
            pltpu.VMEM((KEYS, HD), F32),
            pltpu.VMEM((QB, HD, ROWS), F32),
            pltpu.VMEM((QB, ROWS), F32),
            pltpu.VMEM((QB, ROWS), F32),
            INFO,
            pltpu.VMEM((CH, ROWS), BF16),
            pltpu.VMEM((CH, ROWS), BF16),
        ],
        5 * rows * KEYS * HD,
    )(meta, *args)


def on_device(query_states, key_states, value_states, output_grad, positions):
    own_ids = (positions[::SPAN] // SPAN).astype(BF16)
    kv = jnp.concatenate(
        [
            jnp.concatenate([key_states, value_states], axis=1),
            jnp.broadcast_to(jnp.repeat(own_ids, HD)[None, :], (16, 2 * HD)),
        ],
        axis=0,
    )
    qg = jnp.concatenate(
        [
            query_states,
            jnp.broadcast_to(jnp.repeat(own_ids, 4 * HD)[None, :], (16, HQ * HD)),
            output_grad,
        ],
        axis=0,
    )
    qg, kv = lax.optimization_barrier((qg, kv))
    qa = send(qg, along_y(1))
    qb = send(qg, along_y(-1))
    pair = jnp.concatenate([kv, send(kv, to_core)], axis=0)
    second = send(pair, along_z(2))
    first = send(pair, along_z(1))
    first, second, qa, qb = lax.optimization_barrier((first, second, qa, qb))
    qc = send(qa[:SHARD], along_y(1))
    gc = send(qb[SHARD:], along_y(-1))
    far = send(second[:SHARD], along_z(2))
    third = send(second, along_z(1))
    ka = jnp.concatenate([first, second, third, far], axis=0)
    ka, qc, gc = lax.optimization_barrier((ka, qc, gc))
    kx = send(ka, to_core)

    def ids_of(x):
        return x.reshape(-1, SHARD, 2 * HD)[:, TOK, ::HD].reshape(-1)

    kid = jnp.concatenate([ids_of(pair), ids_of(ka), ids_of(kx)]).astype(jnp.int32)
    qid = jnp.concatenate(
        [own_ids] + [x[TOK, :: 4 * HD] for x in (qa, qb, qc)]
    ).astype(jnp.int32)
    rank = jnp.sum((kid[None, :] < kid[:, None]).astype(jnp.int32), axis=1)
    slots = jnp.arange(KB, dtype=jnp.int32)
    in_order = jnp.sum(jnp.where(rank[None, :] == slots[:, None], kid[None, :], 0), axis=1)
    upto = jnp.sum((kid[None, :] <= qid[:, None]).astype(jnp.int32), axis=1)
    per = CH // SPAN
    meta = jnp.concatenate([rank, in_order, (upto + per - 1) // per, qid])

    args = (pair, ka, kx, query_states, output_grad, qa, qb, qc, gc)
    st = fwd_call(meta, *args)
    stats = (st, send(st, along_y(1)), send(st, along_y(-1)), send(st, along_y(2)))
    dq, here, away = bwd_call(meta, *args, *stats)

    terms = [dq[0], send(dq[3], along_y(2)), send(dq[1], along_y(-1)), send(dq[2], along_y(1))]
    query_grad = sum(t.astype(F32) for t in terms).astype(BF16)
    both = here.astype(F32) + send(away, to_core).astype(F32)
    out = both[TOK:].astype(BF16)
    back = [send(out[(2 * d - 2) * TOK:2 * d * TOK], along_z(-d)) for d in (3, 2, 1)]
    back_far = send(out[6 * TOK:], along_z(-4))
    found = sum(t.astype(F32) for t in back)
    cross = send(found[TOK:].astype(BF16), to_core)
    pair_grad = both[:TOK] + back_far.astype(F32) + found[:TOK] + cross.astype(F32)
    return (
        query_grad,
        pair_grad[:, :HD].astype(BF16),
        pair_grad[:, HD:].astype(BF16),
    )


def solution(mesh):
    in_specs = (
        P(("inner", "outer"), "heads"),
        P(("inner", "outer"), "heads"),
        P(("inner", "outer"), "heads"),
        P(("inner", "outer"), "heads"),
        P(("inner", "outer")),
    )
    out_specs = (
        P(("inner", "outer"), "heads"),
        P(("inner", "outer"), "heads"),
        P(("inner", "outer"), "heads"),
    )
    return jax.shard_map(
        on_device, mesh=mesh, in_specs=in_specs, out_specs=out_specs, check_vma=False
    )
```

```python
import functools

import jax
import jax.numpy as jnp
from jax import lax
from jax.experimental import pallas as pl
from jax.experimental.pallas import tpu as pltpu
from jax.sharding import PartitionSpec as P

F32 = jnp.float32
BF16 = jnp.bfloat16
AXES = ("inner", "outer")
HD = 128
HQ = 8
SPAN = 64
TOK = 128
SHARD = TOK + 16
NZ, NY, NC = 8, 4, 2
ROWS = SPAN * HQ
QB = 2 * NY
KB = 2 * NZ * NC
KEYS = KB * SPAN
CH = 512
PER = CH // SPAN
SCALE = HD ** -0.5
SCALE2 = SCALE * 1.4426950408889634
NEG = -1e30
VMEM_LIMIT = 48 * 1024 * 1024
FROM_BELOW = (2, 0, 3, 1)
FROM_ABOVE = (1, 3, 0, 2)
FROM_FAR = (3, 2, 1, 0)


def flat(z, y, c):
    return ((z % NZ) * NY + y % NY) * NC + c


def moves(fn):
    return [
        (flat(z, y, c), flat(*fn(z, y, c)))
        for z in range(NZ)
        for y in range(NY)
        for c in range(NC)
    ]


def send(x, fn):
    return lax.ppermute(x, AXES, moves(fn))


def to_core(z, y, c):
    return z, y, 1 - c


def along_y(d):
    return lambda z, y, c: (z, y + d, c)


def along_y_by_core(z, y, c):
    return (z, y + 1 if c == 0 else y - 1, c)


def along_z(d):
    return lambda z, y, c: (z + d if c == 0 else z - d, y, c)


def dot_nt(a, b):
    return lax.dot_general(a, b, (((1,), (1,)), ((), ())), preferred_element_type=F32)


def dot_nn(a, b):
    return lax.dot_general(a, b, (((1,), (0,)), ((), ())), preferred_element_type=F32)


def key_shards(refs):
    for ref in refs:
        for i in range(ref.shape[0] // SHARD):
            yield ref, i


def sort_keys(meta, refs, ks, vs):
    for s, (ref, i) in enumerate(key_shards(refs)):
        for b in range(2):
            row = i * SHARD + b * SPAN
            dst = pl.ds(pl.multiple_of(meta[2 * s + b] * SPAN, SPAN), SPAN)
            ks[dst, :] = ref[row:row + SPAN, 0:HD]
            vs[dst, :] = ref[row:row + SPAN, HD:2 * HD]


def fill_rows(parts, out):
    for r, (ref, row) in enumerate(parts):
        for b in range(2):
            for h in range(HQ):
                at = ((r * 2 + b) * HQ + h) * SPAN
                out[at:at + SPAN, :] = ref[row + b * SPAN:row + (b + 1) * SPAN, h * HD:(h + 1) * HD]


def lead():
    u = lax.broadcasted_iota(jnp.int32, (SPAN, ROWS), 0)
    t = lax.broadcasted_iota(jnp.int32, (SPAN, ROWS), 1) % SPAN
    return u - t


def masked(meta, scores, diff, first, qid, fill):
    parts = []
    for b in range(scores.shape[0] // SPAN):
        gap = (qid - meta[KB + first + b]) * SPAN
        part = scores[b * SPAN:(b + 1) * SPAN, :]
        parts.append(jnp.where(diff <= gap, part, fill))
    return jnp.concatenate(parts, axis=0)


def walk(meta, qb, step):
    whole = meta[2 * KB + qb]
    halves = meta[2 * KB + QB + qb]
    fulls = meta[2 * KB + 2 * QB + qb]
    lax.fori_loop(0, whole, lambda j, _: step(j * PER, CH, False), 0)
    lax.fori_loop(0, halves, lambda j, _: step(whole * PER, CH // 2, True), 0)
    lax.fori_loop(0, fulls, lambda j, _: step(whole * PER, CH, True), 0)


def query_rows(qb):
    return pl.ds(pl.multiple_of(qb * ROWS, ROWS), ROWS)


def key_rows(first, size):
    return pl.ds(pl.multiple_of(first * SPAN, CH), size)


def forward_kernel(
    meta, own, ka, kb, xa, xb, q0, g0, qa, qb, qc, st,
    ks, vs, vt, qs, gs, gt, past, sc, ex, mx, hi,
):
    sort_keys(meta, (own, ka, kb, xa, xb), ks, vs)
    for j in range(KEYS // HD):
        vt[0:HD, j * HD:(j + 1) * HD] = vs[j * HD:(j + 1) * HD, :].T
    vt[HD:HD + 16, :] = jnp.ones((16, KEYS), BF16)
    fill_rows(((q0, 0), (qa, 0), (qb, 0), (qc, 0)), qs)
    fill_rows(((g0, 0), (qa, SHARD), (qb, SHARD), (qc, SHARD)), gs)
    for j in range(QB):
        gt[j, :, :] = gs[j * ROWS:(j + 1) * ROWS, :].T
    st[0, :, :] = jnp.full((QB, ROWS), NEG, F32)
    st[1, :, :] = jnp.zeros((QB, ROWS), F32)
    st[2, :, :] = jnp.zeros((QB, ROWS), F32)
    sc[...] = jnp.full_like(sc, NEG)
    ex[...] = jnp.zeros_like(ex)
    mx[...] = jnp.full_like(mx, NEG)
    hi[...] = jnp.full_like(hi, NEG)
    for i in range(4):
        past[i] = 0
    diff = lead()

    def finish(qb, first):
        acc = dot_nn(vt[:, key_rows(first, CH)], ex[...])
        total = acc[HD:HD + 1, :]
        dots = jnp.sum(gt[qb].astype(F32) * acc[0:HD, :], axis=0, keepdims=True)
        row = pl.ds(qb, 1)
        peak, old = mx[...], st[0, row, :]
        top = jnp.maximum(peak, old)
        new_w, old_w = jnp.exp2(peak - top), jnp.exp2(old - top)
        st[0, row, :] = top
        st[1, row, :] = st[1, row, :] * old_w + total * new_w
        st[2, row, :] = st[2, row, :] * old_w + dots * new_w

    def weigh():
        peak = jnp.max(hi[...], axis=0, keepdims=True)
        mx[...] = peak
        ex[...] = jnp.exp2(sc[...] - peak).astype(BF16)

    def block(qb, _):
        qid = meta[2 * KB + 3 * QB + qb]

        def step(first, size, mask):
            finish(past[0], past[1])
            weigh()
            s = dot_nt(ks[key_rows(first, size), :], qs[query_rows(qb), :]) * SCALE2
            if mask:
                s = masked(meta, s, diff, first, qid, NEG)
            sc[0:size, :] = s
            if size < CH:
                sc[size:CH, :] = jnp.full((CH - size, ROWS), NEG, F32)
            hi[...] = jnp.max(s.reshape(size // 8, 8, ROWS), axis=0)
            past[0] = past[2]
            past[1] = past[3]
            past[2] = qb
            past[3] = first
            return 0

        walk(meta, qb, step)
        return 0

    lax.fori_loop(0, QB, block, 0)
    finish(past[0], past[1])
    weigh()
    finish(past[2], past[3])


def regroup(x, order):
    return jnp.concatenate([x[2 * i:2 * i + 2, :] for i in order], axis=0)


def backward_kernel(
    meta, own, ka, kb, xa, xb, q0, g0, qa, qb, qc, st0, sta, stb, stc,
    dq, dhere, daway, ks, vs, kt, qs, gs, dk, dv, qacc, lse, dlt,
):
    sort_keys(meta, (own, ka, kb, xa, xb), ks, vs)
    for j in range(KEYS // HD):
        kt[:, j * HD:(j + 1) * HD] = ks[j * HD:(j + 1) * HD, :].T
    fill_rows(((q0, 0), (qa, 0), (qb, 0), (qc, 0)), qs)
    fill_rows(((g0, 0), (qa, SHARD), (qb, SHARD), (qc, SHARD)), gs)
    same = (0, 1, 2, 3)
    sources = ((st0, same), (sta, FROM_BELOW), (stb, FROM_ABOVE), (stc, FROM_FAR))
    peaks = [regroup(s[0], o) for s, o in sources]
    top = functools.reduce(jnp.maximum, peaks)
    shares = [jnp.exp2(p - top) for p in peaks]
    total = sum(w * regroup(s[1], o) for w, (s, o) in zip(shares, sources))
    dots = sum(w * regroup(s[2], o) for w, (s, o) in zip(shares, sources))
    lse[...] = top + jnp.log2(total)
    dlt[...] = dots / total
    for ref in (dk, dv, qacc):
        ref[...] = jnp.zeros_like(ref)
    diff = lead()

    def block(qb, _):
        rows = query_rows(qb)
        q, g = qs[rows, :], gs[rows, :]
        row_lse, row_dlt = lse[pl.ds(qb, 1), :], dlt[pl.ds(qb, 1), :]
        qid = meta[2 * KB + 3 * QB + qb]

        def step(first, size, mask):
            at = key_rows(first, size)
            p = jnp.exp2(dot_nt(ks[at, :], q) * SCALE2 - row_lse)
            if mask:
                p = masked(meta, p, diff, first, qid, 0.0)
            ds = (p * (dot_nt(vs[at, :], g) - row_dlt)).astype(BF16)
            dv[at, :] += dot_nn(p.astype(BF16), g)
            dk[at, :] += dot_nn(ds, q)
            qacc[qb] += dot_nn(kt[:, at], ds)
            return 0

        walk(meta, qb, step)
        return 0

    lax.fori_loop(0, QB, block, 0)
    for i in range(QB):
        done = (qacc[i] * SCALE).T.astype(BF16)
        for h in range(HQ):
            row = (i % 2) * SPAN
            dq[i // 2, row:row + SPAN, h * HD:(h + 1) * HD] = done[h * SPAN:(h + 1) * SPAN, :]
    for s in range(2 * NZ):
        for b in range(2):
            src = pl.ds(pl.multiple_of(meta[2 * s + b] * SPAN, SPAN), SPAN)
            if s == 0:
                ref, i = dhere, 0
            elif s == 1:
                ref, i = daway, 0
            elif s < 9:
                ref, i = dhere, s - 1
            else:
                ref, i = daway, s - 8
            row = i * TOK + b * SPAN
            ref[row:row + SPAN, 0:HD] = (dk[src, :] * SCALE).astype(BF16)
            ref[row:row + SPAN, HD:2 * HD] = dv[src, :].astype(BF16)


def call(body, outs, scratch, flops):
    vmem = pl.BlockSpec(memory_space=pltpu.VMEM)
    smem = pl.BlockSpec(memory_space=pltpu.SMEM)

    def run(meta, *args):
        return pl.pallas_call(
            body,
            out_shape=outs,
            in_specs=[smem] + [vmem] * len(args),
            out_specs=jax.tree.map(lambda _: vmem, outs),
            scratch_shapes=scratch,
            compiler_params=pltpu.CompilerParams(vmem_limit_bytes=VMEM_LIMIT),
            cost_estimate=pl.CostEstimate(
                flops=flops, bytes_accessed=6 * 1024 * 1024, transcendentals=QB * ROWS * KEYS // 2
            ),
        )(meta, *args)

    return run


def shape(*dims, dtype=BF16):
    return jax.ShapeDtypeStruct(dims, dtype)


def fwd_call(meta, *args):
    rows = QB * ROWS
    return call(
        forward_kernel,
        shape(3, QB, ROWS, dtype=F32),
        [
            pltpu.VMEM((KEYS, HD), BF16),
            pltpu.VMEM((KEYS, HD), BF16),
            pltpu.VMEM((HD + 16, KEYS), BF16),
            pltpu.VMEM((rows, HD), BF16),
            pltpu.VMEM((rows, HD), BF16),
            pltpu.VMEM((QB, HD, ROWS), BF16),
            pltpu.SMEM((4,), jnp.int32),
            pltpu.VMEM((CH, ROWS), F32),
            pltpu.VMEM((CH, ROWS), BF16),
            pltpu.VMEM((1, ROWS), F32),
            pltpu.VMEM((8, ROWS), F32),
        ],
        2 * rows * KEYS * HD,
    )(meta, *args)


def bwd_call(meta, *args):
    rows = QB * ROWS
    return call(
        backward_kernel,
        (shape(NY, TOK, HQ * HD), shape(8 * TOK, 2 * HD), shape(8 * TOK, 2 * HD)),
        [
            pltpu.VMEM((KEYS, HD), BF16),
            pltpu.VMEM((KEYS, HD), BF16),
            pltpu.VMEM((HD, KEYS), BF16),
            pltpu.VMEM((rows, HD), BF16),
            pltpu.VMEM((rows, HD), BF16),
            pltpu.VMEM((KEYS, HD), F32),
            pltpu.VMEM((KEYS, HD), F32),
            pltpu.VMEM((QB, HD, ROWS), F32),
            pltpu.VMEM((QB, ROWS), F32),
            pltpu.VMEM((QB, ROWS), F32),
        ],
        5 * rows * KEYS * HD,
    )(meta, *args)


def on_device(query_states, key_states, value_states, output_grad, positions):
    own_ids = (positions[::SPAN] // SPAN).astype(BF16)
    kv = jnp.concatenate(
        [
            jnp.concatenate([key_states, value_states], axis=1),
            jnp.broadcast_to(jnp.repeat(own_ids, HD)[None, :], (16, 2 * HD)),
        ],
        axis=0,
    )
    qg = jnp.concatenate(
        [
            query_states,
            jnp.broadcast_to(jnp.repeat(own_ids, 4 * HD)[None, :], (16, HQ * HD)),
            output_grad,
        ],
        axis=0,
    )
    qg, kv = lax.optimization_barrier((qg, kv))
    qa = send(qg, along_y(1))
    qb = send(qg, along_y(-1))
    pair = jnp.concatenate([kv, send(kv, to_core)], axis=0)
    third = send(pair, along_z(3))
    first = send(pair, along_z(1))
    qa, qb, first, third = lax.optimization_barrier((qa, qb, first, third))
    lower = lax.axis_index("outer") % NC == 0
    qc = send(jnp.where(lower, qa, qb), along_y_by_core)
    kb = send(jnp.concatenate([first, third[:SHARD]], axis=0), along_z(1))
    ka = jnp.concatenate([first, third], axis=0)
    xa = send(ka, to_core)
    kb, qc = lax.optimization_barrier((kb, qc))
    xb = send(kb, to_core)

    def ids_of(x):
        return x.reshape(-1, SHARD, 2 * HD)[:, TOK, ::HD].reshape(-1)

    kid = jnp.concatenate([ids_of(x) for x in (pair, ka, kb, xa, xb)]).astype(jnp.int32)
    qid = jnp.concatenate(
        [own_ids] + [x[TOK, :: 4 * HD] for x in (qa, qb, qc)]
    ).astype(jnp.int32)
    rank = jnp.sum((kid[None, :] < kid[:, None]).astype(jnp.int32), axis=1)
    slots = jnp.arange(KB, dtype=jnp.int32)
    in_order = jnp.sum(jnp.where(rank[None, :] == slots[:, None], kid[None, :], 0), axis=1)
    below = jnp.sum((kid[None, :] < qid[:, None]).astype(jnp.int32), axis=1)
    upto = jnp.sum((kid[None, :] <= qid[:, None]).astype(jnp.int32), axis=1)
    whole = below // PER
    left = upto - whole * PER
    halves = ((left > 0) & (left <= PER // 2)).astype(jnp.int32)
    fulls = (left > PER // 2).astype(jnp.int32)
    meta = jnp.concatenate([rank, in_order, whole, halves, fulls, qid])

    args = (pair, ka, kb, xa, xb, query_states, output_grad, qa, qb, qc)
    st = fwd_call(meta, *args)
    stats = (st, send(st, along_y(1)), send(st, along_y(-1)), send(st, along_y(2)))
    dq, here, away = bwd_call(meta, *args, *stats)

    terms = [dq[0], send(dq[3], along_y(2)), send(dq[1], along_y(-1)), send(dq[2], along_y(1))]
    query_grad = sum(t.astype(F32) for t in terms).astype(BF16)
    both = here.astype(F32) + send(away, to_core).astype(F32)
    out = both[TOK:].astype(BF16)
    back = [
        send(out[2 * TOK:4 * TOK], along_z(-3)),
        send(out[4 * TOK:6 * TOK], along_z(-2)),
        send(out[:2 * TOK], along_z(-1)),
    ]
    back_far = send(out[6 * TOK:], along_z(-4))
    found = sum(t.astype(F32) for t in back)
    cross = send(found[TOK:].astype(BF16), to_core)
    pair_grad = both[:TOK] + back_far.astype(F32) + found[:TOK] + cross.astype(F32)
    return (
        query_grad,
        pair_grad[:, :HD].astype(BF16),
        pair_grad[:, HD:].astype(BF16),
    )


def solution(mesh):
    in_specs = (
        P(("inner", "outer"), "heads"),
        P(("inner", "outer"), "heads"),
        P(("inner", "outer"), "heads"),
        P(("inner", "outer"), "heads"),
        P(("inner", "outer")),
    )
    out_specs = (
        P(("inner", "outer"), "heads"),
        P(("inner", "outer"), "heads"),
        P(("inner", "outer"), "heads"),
    )
    return jax.shard_map(
        on_device, mesh=mesh, in_specs=in_specs, out_specs=out_specs, check_vma=False
    )
```

```python
import functools

import jax
import jax.numpy as jnp
from jax import lax
from jax.experimental import pallas as pl
from jax.experimental.pallas import tpu as pltpu
from jax.sharding import PartitionSpec as P

F32 = jnp.float32
BF16 = jnp.bfloat16
AXES = ("inner", "outer")
HD = 128
HQ = 8
SPAN = 64
TOK = 128
SHARD = TOK + 16
NZ, NY, NC = 8, 4, 2
ROWS = SPAN * HQ
QB = 2 * NY
KB = 2 * NZ * NC
KEYS = KB * SPAN
CH = 512
PER = CH // SPAN
SCALE = HD ** -0.5
SCALE2 = SCALE * 1.4426950408889634
NEG = -1e30
VMEM_LIMIT = 48 * 1024 * 1024
FROM_BELOW = (2, 0, 3, 1)
FROM_ABOVE = (1, 3, 0, 2)
FROM_FAR = (3, 2, 1, 0)


def flat(z, y, c):
    return ((z % NZ) * NY + y % NY) * NC + c


def moves(fn):
    return [
        (flat(z, y, c), flat(*fn(z, y, c)))
        for z in range(NZ)
        for y in range(NY)
        for c in range(NC)
    ]


def send(x, fn):
    return lax.ppermute(x, AXES, moves(fn))


def to_core(z, y, c):
    return z, y, 1 - c


def along_y(d):
    return lambda z, y, c: (z, y + d, c)


def along_y_by_core(z, y, c):
    return (z, y + 1 if c == 0 else y - 1, c)


def along_z(d):
    return lambda z, y, c: (z + d if c == 0 else z - d, y, c)


def dot_nt(a, b):
    return lax.dot_general(a, b, (((1,), (1,)), ((), ())), preferred_element_type=F32)


def dot_nn(a, b):
    return lax.dot_general(a, b, (((1,), (0,)), ((), ())), preferred_element_type=F32)


def key_shards(refs):
    for ref in refs:
        for i in range(ref.shape[0] // SHARD):
            yield ref, i


def sort_keys(meta, refs, ks, vs):
    for s, (ref, i) in enumerate(key_shards(refs)):
        for b in range(2):
            row = i * SHARD + b * SPAN
            dst = pl.ds(pl.multiple_of(meta[2 * s + b] * SPAN, SPAN), SPAN)
            ks[dst, :] = ref[row:row + SPAN, 0:HD]
            vs[dst, :] = ref[row:row + SPAN, HD:2 * HD]


def fill_rows(parts, out):
    for r, (ref, row) in enumerate(parts):
        for b in range(2):
            for h in range(HQ):
                at = ((r * 2 + b) * HQ + h) * SPAN
                out[at:at + SPAN, :] = ref[row + b * SPAN:row + (b + 1) * SPAN, h * HD:(h + 1) * HD]


def lead():
    u = lax.broadcasted_iota(jnp.int32, (SPAN, ROWS), 0)
    t = lax.broadcasted_iota(jnp.int32, (SPAN, ROWS), 1) % SPAN
    return u - t


def masked(meta, scores, diff, first, qid, fill):
    parts = []
    for b in range(scores.shape[0] // SPAN):
        gap = (qid - meta[KB + first + b]) * SPAN
        part = scores[b * SPAN:(b + 1) * SPAN, :]
        parts.append(jnp.where(diff <= gap, part, fill))
    return jnp.concatenate(parts, axis=0)


def walk(meta, qb, step):
    whole = meta[2 * KB + qb]
    halves = meta[2 * KB + QB + qb]
    fulls = meta[2 * KB + 2 * QB + qb]
    lax.fori_loop(0, whole, lambda j, _: step(j * PER, CH, False), 0)
    lax.fori_loop(0, halves, lambda j, _: step(whole * PER, CH // 2, True), 0)
    lax.fori_loop(0, fulls, lambda j, _: step(whole * PER, CH, True), 0)


def walk_wide(meta, qb, step):
    whole = meta[2 * KB + qb]
    halves = meta[2 * KB + QB + qb]
    fulls = meta[2 * KB + 2 * QB + qb]
    lax.fori_loop(0, whole // 2, lambda j, _: step(j * 2 * PER, 2 * CH, False), 0)
    lax.fori_loop(0, whole % 2, lambda j, _: step((whole - 1) * PER, CH, False), 0)
    lax.fori_loop(0, halves, lambda j, _: step(whole * PER, CH // 2, True), 0)
    lax.fori_loop(0, fulls, lambda j, _: step(whole * PER, CH, True), 0)


def query_rows(qb):
    return pl.ds(pl.multiple_of(qb * ROWS, ROWS), ROWS)


def key_rows(first, size):
    return pl.ds(pl.multiple_of(first * SPAN, CH), size)


def forward_kernel(
    meta, own, ka, kb, xa, xb, q0, g0, qa, qb, qc, st,
    ks, vs, vt, qs, gs, gt, past, sc, ex, mx, hi,
):
    sort_keys(meta, (own, ka, kb, xa, xb), ks, vs)
    for j in range(KEYS // HD):
        vt[0:HD, j * HD:(j + 1) * HD] = vs[j * HD:(j + 1) * HD, :].T
    vt[HD:HD + 16, :] = jnp.ones((16, KEYS), BF16)
    fill_rows(((q0, 0), (qa, 0), (qb, 0), (qc, 0)), qs)
    fill_rows(((g0, 0), (qa, SHARD), (qb, SHARD), (qc, SHARD)), gs)
    for j in range(QB):
        gt[j, :, :] = gs[j * ROWS:(j + 1) * ROWS, :].T
    st[0, :, :] = jnp.full((QB, ROWS), NEG, F32)
    st[1, :, :] = jnp.zeros((QB, ROWS), F32)
    st[2, :, :] = jnp.zeros((QB, ROWS), F32)
    sc[...] = jnp.full_like(sc, NEG)
    ex[...] = jnp.zeros_like(ex)
    mx[...] = jnp.full_like(mx, NEG)
    hi[...] = jnp.full_like(hi, NEG)
    for i in range(4):
        past[i] = 0
    diff = lead()

    def finish(qb, first):
        acc = dot_nn(vt[:, key_rows(first, CH)], ex[...])
        total = acc[HD:HD + 1, :]
        dots = jnp.sum(gt[qb].astype(F32) * acc[0:HD, :], axis=0, keepdims=True)
        row = pl.ds(qb, 1)
        peak, old = mx[...], st[0, row, :]
        top = jnp.maximum(peak, old)
        new_w, old_w = jnp.exp2(peak - top), jnp.exp2(old - top)
        st[0, row, :] = top
        st[1, row, :] = st[1, row, :] * old_w + total * new_w
        st[2, row, :] = st[2, row, :] * old_w + dots * new_w

    def weigh():
        peak = jnp.max(hi[...], axis=0, keepdims=True)
        mx[...] = peak
        ex[...] = jnp.exp2(sc[...] - peak).astype(BF16)

    def block(qb, _):
        qid = meta[2 * KB + 3 * QB + qb]

        def step(first, size, mask):
            finish(past[0], past[1])
            weigh()
            s = dot_nt(ks[key_rows(first, size), :], qs[query_rows(qb), :]) * SCALE2
            if mask:
                s = masked(meta, s, diff, first, qid, NEG)
            sc[0:size, :] = s
            if size < CH:
                sc[size:CH, :] = jnp.full((CH - size, ROWS), NEG, F32)
            hi[...] = jnp.max(s.reshape(size // 8, 8, ROWS), axis=0)
            past[0] = past[2]
            past[1] = past[3]
            past[2] = qb
            past[3] = first
            return 0

        walk(meta, qb, step)
        return 0

    lax.fori_loop(0, QB, block, 0)
    finish(past[0], past[1])
    weigh()
    finish(past[2], past[3])


def regroup(x, order):
    return jnp.concatenate([x[2 * i:2 * i + 2, :] for i in order], axis=0)


def backward_kernel(
    meta, own, ka, kb, xa, xb, q0, g0, qa, qb, qc, st0, sta, stb, stc,
    dq, dhere, daway, ks, vs, kt, qs, gs, dk, dv, qacc, lse, dlt,
):
    sort_keys(meta, (own, ka, kb, xa, xb), ks, vs)
    for j in range(KEYS // HD):
        kt[:, j * HD:(j + 1) * HD] = ks[j * HD:(j + 1) * HD, :].T
    fill_rows(((q0, 0), (qa, 0), (qb, 0), (qc, 0)), qs)
    fill_rows(((g0, 0), (qa, SHARD), (qb, SHARD), (qc, SHARD)), gs)
    same = (0, 1, 2, 3)
    sources = ((st0, same), (sta, FROM_BELOW), (stb, FROM_ABOVE), (stc, FROM_FAR))
    peaks = [regroup(s[0], o) for s, o in sources]
    top = functools.reduce(jnp.maximum, peaks)
    shares = [jnp.exp2(p - top) for p in peaks]
    total = sum(w * regroup(s[1], o) for w, (s, o) in zip(shares, sources))
    dots = sum(w * regroup(s[2], o) for w, (s, o) in zip(shares, sources))
    lse[...] = top + jnp.log2(total)
    dlt[...] = dots / total
    for ref in (dk, dv, qacc):
        ref[...] = jnp.zeros_like(ref)
    diff = lead()

    def block(qb, _):
        rows = query_rows(qb)
        q, g = qs[rows, :], gs[rows, :]
        row_lse, row_dlt = lse[pl.ds(qb, 1), :], dlt[pl.ds(qb, 1), :]
        qid = meta[2 * KB + 3 * QB + qb]

        def step(first, size, mask):
            at = key_rows(first, size)
            p = jnp.exp2(dot_nt(ks[at, :], q) * SCALE2 - row_lse)
            if mask:
                p = masked(meta, p, diff, first, qid, 0.0)
            ds = (p * (dot_nt(vs[at, :], g) - row_dlt)).astype(BF16)
            dv[at, :] += dot_nn(p.astype(BF16), g)
            dk[at, :] += dot_nn(ds, q)
            qacc[qb] += dot_nn(kt[:, at], ds)
            return 0

        walk_wide(meta, qb, step)
        return 0

    lax.fori_loop(0, QB, block, 0)
    for i in range(QB):
        done = (qacc[i] * SCALE).T.astype(BF16)
        for h in range(HQ):
            row = (i % 2) * SPAN
            dq[i // 2, row:row + SPAN, h * HD:(h + 1) * HD] = done[h * SPAN:(h + 1) * SPAN, :]
    for s in range(2 * NZ):
        for b in range(2):
            src = pl.ds(pl.multiple_of(meta[2 * s + b] * SPAN, SPAN), SPAN)
            if s == 0:
                ref, i = dhere, 0
            elif s == 1:
                ref, i = daway, 0
            elif s < 9:
                ref, i = dhere, s - 1
            else:
                ref, i = daway, s - 8
            row = i * TOK + b * SPAN
            ref[row:row + SPAN, 0:HD] = (dk[src, :] * SCALE).astype(BF16)
            ref[row:row + SPAN, HD:2 * HD] = dv[src, :].astype(BF16)


def call(body, outs, scratch, flops):
    vmem = pl.BlockSpec(memory_space=pltpu.VMEM)
    smem = pl.BlockSpec(memory_space=pltpu.SMEM)

    def run(meta, *args):
        return pl.pallas_call(
            body,
            out_shape=outs,
            in_specs=[smem] + [vmem] * len(args),
            out_specs=jax.tree.map(lambda _: vmem, outs),
            scratch_shapes=scratch,
            compiler_params=pltpu.CompilerParams(vmem_limit_bytes=VMEM_LIMIT),
            cost_estimate=pl.CostEstimate(
                flops=flops, bytes_accessed=6 * 1024 * 1024, transcendentals=QB * ROWS * KEYS // 2
            ),
        )(meta, *args)

    return run


def shape(*dims, dtype=BF16):
    return jax.ShapeDtypeStruct(dims, dtype)


def fwd_call(meta, *args):
    rows = QB * ROWS
    return call(
        forward_kernel,
        shape(3, QB, ROWS, dtype=F32),
        [
            pltpu.VMEM((KEYS, HD), BF16),
            pltpu.VMEM((KEYS, HD), BF16),
            pltpu.VMEM((HD + 16, KEYS), BF16),
            pltpu.VMEM((rows, HD), BF16),
            pltpu.VMEM((rows, HD), BF16),
            pltpu.VMEM((QB, HD, ROWS), BF16),
            pltpu.SMEM((4,), jnp.int32),
            pltpu.VMEM((CH, ROWS), F32),
            pltpu.VMEM((CH, ROWS), BF16),
            pltpu.VMEM((1, ROWS), F32),
            pltpu.VMEM((8, ROWS), F32),
        ],
        2 * rows * KEYS * HD,
    )(meta, *args)


def bwd_call(meta, *args):
    rows = QB * ROWS
    return call(
        backward_kernel,
        (shape(NY, TOK, HQ * HD), shape(8 * TOK, 2 * HD), shape(8 * TOK, 2 * HD)),
        [
            pltpu.VMEM((KEYS, HD), BF16),
            pltpu.VMEM((KEYS, HD), BF16),
            pltpu.VMEM((HD, KEYS), BF16),
            pltpu.VMEM((rows, HD), BF16),
            pltpu.VMEM((rows, HD), BF16),
            pltpu.VMEM((KEYS, HD), F32),
            pltpu.VMEM((KEYS, HD), F32),
            pltpu.VMEM((QB, HD, ROWS), F32),
            pltpu.VMEM((QB, ROWS), F32),
            pltpu.VMEM((QB, ROWS), F32),
        ],
        5 * rows * KEYS * HD,
    )(meta, *args)


def on_device(query_states, key_states, value_states, output_grad, positions):
    ids = (positions // SPAN).astype(BF16)
    kv = jnp.concatenate(
        [
            jnp.concatenate([key_states, value_states], axis=1),
            jnp.broadcast_to(jnp.tile(ids, 2)[None, :], (16, 2 * HD)),
        ],
        axis=0,
    )
    qg = jnp.concatenate(
        [
            query_states,
            jnp.broadcast_to(jnp.tile(ids, HQ)[None, :], (16, HQ * HD)),
            output_grad,
        ],
        axis=0,
    )
    qg, kv = lax.optimization_barrier((qg, kv))
    qa = send(qg, along_y(1))
    qb = send(qg, along_y(-1))
    pair = jnp.concatenate([kv, send(kv, to_core)], axis=0)
    third = send(pair, along_z(3))
    first = send(pair, along_z(1))
    qa, qb, first, third = lax.optimization_barrier((qa, qb, first, third))
    lower = lax.axis_index("outer") % NC == 0
    qc = send(jnp.where(lower, qa, qb), along_y_by_core)
    kb = send(jnp.concatenate([first, third[:SHARD]], axis=0), along_z(1))
    ka = jnp.concatenate([first, third], axis=0)
    xa = send(ka, to_core)
    kb, qc = lax.optimization_barrier((kb, qc))
    xb = send(kb, to_core)

    def ids_of(x):
        return x.reshape(-1, SHARD, 2 * HD)[:, TOK, 0:HD:SPAN].reshape(-1)

    kid = jnp.concatenate([ids_of(x) for x in (pair, ka, kb, xa, xb)]).astype(jnp.int32)
    qid = jnp.concatenate([ids[::SPAN]] + [x[TOK, 0:HD:SPAN] for x in (qa, qb, qc)]).astype(jnp.int32)
    rank = jnp.sum((kid[None, :] < kid[:, None]).astype(jnp.int32), axis=1)
    slots = jnp.arange(KB, dtype=jnp.int32)
    in_order = jnp.sum(jnp.where(rank[None, :] == slots[:, None], kid[None, :], 0), axis=1)
    below = jnp.sum((kid[None, :] < qid[:, None]).astype(jnp.int32), axis=1)
    upto = jnp.sum((kid[None, :] <= qid[:, None]).astype(jnp.int32), axis=1)
    whole = below // PER
    left = upto - whole * PER
    halves = ((left > 0) & (left <= PER // 2)).astype(jnp.int32)
    fulls = (left > PER // 2).astype(jnp.int32)
    meta = jnp.concatenate([rank, in_order, whole, halves, fulls, qid])

    args = (pair, ka, kb, xa, xb, query_states, output_grad, qa, qb, qc)
    st = fwd_call(meta, *args)
    stats = (st, send(st, along_y(1)), send(st, along_y(-1)), send(st, along_y(2)))
    dq, here, away = bwd_call(meta, *args, *stats)

    terms = [dq[0], send(dq[3], along_y(2)), send(dq[1], along_y(-1)), send(dq[2], along_y(1))]
    query_grad = sum(t.astype(F32) for t in terms).astype(BF16)
    both = here.astype(F32) + send(away, to_core).astype(F32)
    out = both[TOK:].astype(BF16)
    back = [
        send(out[2 * TOK:4 * TOK], along_z(-3)),
        send(out[4 * TOK:6 * TOK], along_z(-2)),
        send(out[:2 * TOK], along_z(-1)),
    ]
    back_far = send(out[6 * TOK:], along_z(-4))
    found = sum(t.astype(F32) for t in back)
    cross = send(found[TOK:].astype(BF16), to_core)
    pair_grad = both[:TOK] + back_far.astype(F32) + found[:TOK] + cross.astype(F32)
    return (
        query_grad,
        pair_grad[:, :HD].astype(BF16),
        pair_grad[:, HD:].astype(BF16),
    )


def solution(mesh):
    in_specs = (
        P(("inner", "outer"), "heads"),
        P(("inner", "outer"), "heads"),
        P(("inner", "outer"), "heads"),
        P(("inner", "outer"), "heads"),
        P(("inner", "outer")),
    )
    out_specs = (
        P(("inner", "outer"), "heads"),
        P(("inner", "outer"), "heads"),
        P(("inner", "outer"), "heads"),
    )
    return jax.shard_map(
        on_device, mesh=mesh, in_specs=in_specs, out_specs=out_specs, check_vma=False
    )
```

```python
import functools

import jax
import jax.numpy as jnp
from jax import lax
from jax.experimental import pallas as pl
from jax.experimental.pallas import tpu as pltpu
from jax.sharding import PartitionSpec as P

F32 = jnp.float32
BF16 = jnp.bfloat16
AXES = ("inner", "outer")
HD = 128
HQ = 8
SPAN = 64
TOK = 128
SHARD = TOK + 16
NZ, NY, NC = 8, 4, 2
ROWS = SPAN * HQ
QB = 2 * NY
KB = 2 * NZ * NC
KEYS = KB * SPAN
CH = 512
PER = CH // SPAN
SCALE = HD ** -0.5
SCALE2 = SCALE * 1.4426950408889634
NEG = -1e30
VMEM_LIMIT = 48 * 1024 * 1024
PACK_LIMIT = 60 * 1024 * 1024
FROM_BELOW = (2, 0, 3, 1)
FROM_ABOVE = (1, 3, 0, 2)
FROM_FAR = (3, 2, 1, 0)


def flat(z, y, c):
    return ((z % NZ) * NY + y % NY) * NC + c


def moves(fn):
    return [
        (flat(z, y, c), flat(*fn(z, y, c)))
        for z in range(NZ)
        for y in range(NY)
        for c in range(NC)
    ]


def send(x, fn):
    return lax.ppermute(x, AXES, moves(fn))


def to_core(z, y, c):
    return z, y, 1 - c


def along_y(d):
    return lambda z, y, c: (z, y + d, c)


def along_y_by_core(z, y, c):
    return (z, y + 1 if c == 0 else y - 1, c)


def along_z(d):
    return lambda z, y, c: (z + d if c == 0 else z - d, y, c)


def dot_nt(a, b):
    return lax.dot_general(a, b, (((1,), (1,)), ((), ())), preferred_element_type=F32)


def dot_nn(a, b):
    return lax.dot_general(a, b, (((1,), (0,)), ((), ())), preferred_element_type=F32)


def key_shards(refs):
    for ref in refs:
        for i in range(ref.shape[0] // SHARD):
            yield ref, i


def sort_keys(meta, refs, ks, vs):
    for s, (ref, i) in enumerate(key_shards(refs)):
        for b in range(2):
            row = i * SHARD + b * SPAN
            dst = pl.ds(pl.multiple_of(meta[2 * s + b] * SPAN, SPAN), SPAN)
            ks[dst, :] = ref[row:row + SPAN, 0:HD]
            vs[dst, :] = ref[row:row + SPAN, HD:2 * HD]


def fill_rows(parts, out):
    for r, (ref, row) in enumerate(parts):
        for b in range(2):
            for h in range(HQ):
                at = ((r * 2 + b) * HQ + h) * SPAN
                out[at:at + SPAN, :] = ref[row + b * SPAN:row + (b + 1) * SPAN, h * HD:(h + 1) * HD]


def lead():
    u = lax.broadcasted_iota(jnp.int32, (SPAN, ROWS), 0)
    t = lax.broadcasted_iota(jnp.int32, (SPAN, ROWS), 1) % SPAN
    return u - t


def masked(meta, scores, diff, first, qid, fill):
    parts = []
    for b in range(scores.shape[0] // SPAN):
        gap = (qid - meta[KB + first + b]) * SPAN
        part = scores[b * SPAN:(b + 1) * SPAN, :]
        parts.append(jnp.where(diff <= gap, part, fill))
    return jnp.concatenate(parts, axis=0)


def walk(meta, qb, step):
    whole = meta[2 * KB + qb]
    halves = meta[2 * KB + QB + qb]
    fulls = meta[2 * KB + 2 * QB + qb]
    lax.fori_loop(0, whole, lambda j, _: step(j * PER, CH, False), 0)
    lax.fori_loop(0, halves, lambda j, _: step(whole * PER, CH // 2, True), 0)
    lax.fori_loop(0, fulls, lambda j, _: step(whole * PER, CH, True), 0)


def walk_wide(meta, qb, step):
    whole = meta[2 * KB + qb]
    halves = meta[2 * KB + QB + qb]
    fulls = meta[2 * KB + 2 * QB + qb]
    lax.fori_loop(0, whole // 2, lambda j, _: step(j * 2 * PER, 2 * CH, False), 0)
    lax.fori_loop(0, whole % 2, lambda j, _: step((whole - 1) * PER, CH, False), 0)
    lax.fori_loop(0, halves, lambda j, _: step(whole * PER, CH // 2, True), 0)
    lax.fori_loop(0, fulls, lambda j, _: step(whole * PER, CH, True), 0)


def query_rows(qb):
    return pl.ds(pl.multiple_of(qb * ROWS, ROWS), ROWS)


def key_rows(first, size):
    return pl.ds(pl.multiple_of(first * SPAN, CH), size)


def forward_kernel(
    meta, own, ka, kb, xa, xb, q0, g0, qa, qb, qc, st,
    ks, vs, vt, qs, gs, gt, past, sc, ex, mx, hi,
):
    sort_keys(meta, (own, ka, kb, xa, xb), ks, vs)
    for j in range(KEYS // HD):
        vt[0:HD, j * HD:(j + 1) * HD] = vs[j * HD:(j + 1) * HD, :].T
    vt[HD:HD + 16, :] = jnp.ones((16, KEYS), BF16)
    fill_rows(((q0, 0), (qa, 0), (qb, 0), (qc, 0)), qs)
    fill_rows(((g0, 0), (qa, SHARD), (qb, SHARD), (qc, SHARD)), gs)
    for j in range(QB):
        gt[j, :, :] = gs[j * ROWS:(j + 1) * ROWS, :].T
    st[0, :, :] = jnp.full((QB, ROWS), NEG, F32)
    st[1, :, :] = jnp.zeros((QB, ROWS), F32)
    st[2, :, :] = jnp.zeros((QB, ROWS), F32)
    sc[...] = jnp.full_like(sc, NEG)
    ex[...] = jnp.zeros_like(ex)
    mx[...] = jnp.full_like(mx, NEG)
    hi[...] = jnp.full_like(hi, NEG)
    for i in range(4):
        past[i] = 0
    diff = lead()

    def finish(qb, first):
        acc = dot_nn(vt[:, key_rows(first, CH)], ex[...])
        total = acc[HD:HD + 1, :]
        dots = jnp.sum(gt[qb].astype(F32) * acc[0:HD, :], axis=0, keepdims=True)
        row = pl.ds(qb, 1)
        peak, old = mx[...], st[0, row, :]
        top = jnp.maximum(peak, old)
        new_w, old_w = jnp.exp2(peak - top), jnp.exp2(old - top)
        st[0, row, :] = top
        st[1, row, :] = st[1, row, :] * old_w + total * new_w
        st[2, row, :] = st[2, row, :] * old_w + dots * new_w

    def weigh():
        peak = jnp.max(hi[...], axis=0, keepdims=True)
        mx[...] = peak
        ex[...] = jnp.exp2(sc[...] - peak).astype(BF16)

    def block(qb, _):
        qid = meta[2 * KB + 3 * QB + qb]

        def step(first, size, mask):
            finish(past[0], past[1])
            weigh()
            s = dot_nt(ks[key_rows(first, size), :], qs[query_rows(qb), :]) * SCALE2
            if mask:
                s = masked(meta, s, diff, first, qid, NEG)
            sc[0:size, :] = s
            if size < CH:
                sc[size:CH, :] = jnp.full((CH - size, ROWS), NEG, F32)
            hi[...] = jnp.max(s.reshape(size // 8, 8, ROWS), axis=0)
            past[0] = past[2]
            past[1] = past[3]
            past[2] = qb
            past[3] = first
            return 0

        walk(meta, qb, step)
        return 0

    lax.fori_loop(0, QB, block, 0)
    finish(past[0], past[1])
    weigh()
    finish(past[2], past[3])


def regroup(x, order):
    return jnp.concatenate([x[2 * i:2 * i + 2, :] for i in order], axis=0)


def backward_kernel(
    meta, own, ka, kb, xa, xb, q0, g0, qa, qb, qc, st0, sta, stb, stc,
    dq, dhere, daway, ks, vs, kt, qs, gs, dk, dv, qacc, lse, dlt,
):
    sort_keys(meta, (own, ka, kb, xa, xb), ks, vs)
    for j in range(KEYS // HD):
        kt[:, j * HD:(j + 1) * HD] = ks[j * HD:(j + 1) * HD, :].T
    fill_rows(((q0, 0), (qa, 0), (qb, 0), (qc, 0)), qs)
    fill_rows(((g0, 0), (qa, SHARD), (qb, SHARD), (qc, SHARD)), gs)
    same = (0, 1, 2, 3)
    sources = ((st0, same), (sta, FROM_BELOW), (stb, FROM_ABOVE), (stc, FROM_FAR))
    peaks = [regroup(s[0], o) for s, o in sources]
    top = functools.reduce(jnp.maximum, peaks)
    shares = [jnp.exp2(p - top) for p in peaks]
    total = sum(w * regroup(s[1], o) for w, (s, o) in zip(shares, sources))
    dots = sum(w * regroup(s[2], o) for w, (s, o) in zip(shares, sources))
    lse[...] = top + jnp.log2(total)
    dlt[...] = dots / total
    for ref in (dk, dv, qacc):
        ref[...] = jnp.zeros_like(ref)
    diff = lead()

    def block(qb, _):
        rows = query_rows(qb)
        q, g = qs[rows, :], gs[rows, :]
        row_lse, row_dlt = lse[pl.ds(qb, 1), :], dlt[pl.ds(qb, 1), :]
        qid = meta[2 * KB + 3 * QB + qb]

        def step(first, size, mask):
            at = key_rows(first, size)
            p = jnp.exp2(dot_nt(ks[at, :], q) * SCALE2 - row_lse)
            if mask:
                p = masked(meta, p, diff, first, qid, 0.0)
            ds = (p * (dot_nt(vs[at, :], g) - row_dlt)).astype(BF16)
            dv[at, :] += dot_nn(p.astype(BF16), g)
            dk[at, :] += dot_nn(ds, q)
            qacc[qb] += dot_nn(kt[:, at], ds)
            return 0

        walk_wide(meta, qb, step)
        return 0

    lax.fori_loop(0, QB, block, 0)
    for i in range(QB):
        done = (qacc[i] * SCALE).T.astype(BF16)
        for h in range(HQ):
            row = (i % 2) * SPAN
            dq[i // 2, row:row + SPAN, h * HD:(h + 1) * HD] = done[h * SPAN:(h + 1) * SPAN, :]
    for s in range(2 * NZ):
        for b in range(2):
            src = pl.ds(pl.multiple_of(meta[2 * s + b] * SPAN, SPAN), SPAN)
            if s == 0:
                ref, i = dhere, 0
            elif s == 1:
                ref, i = daway, 0
            elif s < 9:
                ref, i = dhere, s - 1
            else:
                ref, i = daway, s - 8
            row = i * TOK + b * SPAN
            ref[row:row + SPAN, 0:HD] = (dk[src, :] * SCALE).astype(BF16)
            ref[row:row + SPAN, HD:2 * HD] = dv[src, :].astype(BF16)


def call(body, outs, scratch, flops, limit=VMEM_LIMIT):
    vmem = pl.BlockSpec(memory_space=pltpu.VMEM)
    smem = pl.BlockSpec(memory_space=pltpu.SMEM)

    def run(meta, *args):
        return pl.pallas_call(
            body,
            out_shape=outs,
            in_specs=[smem] + [vmem] * len(args),
            out_specs=jax.tree.map(lambda _: vmem, outs),
            scratch_shapes=scratch,
            compiler_params=pltpu.CompilerParams(vmem_limit_bytes=limit),
            cost_estimate=pl.CostEstimate(
                flops=flops, bytes_accessed=6 * 1024 * 1024, transcendentals=QB * ROWS * KEYS // 2
            ),
        )(meta, *args)

    return run


def shape(*dims, dtype=BF16):
    return jax.ShapeDtypeStruct(dims, dtype)


def pack_kernel(positions, q, k, v, g, kv, qg):
    def numbers(width):
        lane = lax.broadcasted_iota(jnp.int32, (16, width), 1) % TOK
        first, second = (lax.div(positions[b * SPAN], SPAN) for b in range(2))
        return jnp.where(lane < SPAN, first, second).astype(F32).astype(BF16)

    kv[0:TOK, 0:HD] = k[...]
    kv[0:TOK, HD:2 * HD] = v[...]
    kv[TOK:SHARD, :] = numbers(2 * HD)
    qg[0:TOK, :] = q[...]
    qg[TOK:SHARD, :] = numbers(HQ * HD)
    qg[SHARD:SHARD + TOK, :] = g[...]


def pack_call(*args):
    outs = (shape(SHARD, 2 * HD), shape(SHARD + TOK, HQ * HD))
    return call(pack_kernel, outs, [], 0, PACK_LIMIT)(*args)


def fwd_call(meta, *args):
    rows = QB * ROWS
    return call(
        forward_kernel,
        shape(3, QB, ROWS, dtype=F32),
        [
            pltpu.VMEM((KEYS, HD), BF16),
            pltpu.VMEM((KEYS, HD), BF16),
            pltpu.VMEM((HD + 16, KEYS), BF16),
            pltpu.VMEM((rows, HD), BF16),
            pltpu.VMEM((rows, HD), BF16),
            pltpu.VMEM((QB, HD, ROWS), BF16),
            pltpu.SMEM((4,), jnp.int32),
            pltpu.VMEM((CH, ROWS), F32),
            pltpu.VMEM((CH, ROWS), BF16),
            pltpu.VMEM((1, ROWS), F32),
            pltpu.VMEM((8, ROWS), F32),
        ],
        2 * rows * KEYS * HD,
    )(meta, *args)


def bwd_call(meta, *args):
    rows = QB * ROWS
    return call(
        backward_kernel,
        (shape(NY, TOK, HQ * HD), shape(8 * TOK, 2 * HD), shape(8 * TOK, 2 * HD)),
        [
            pltpu.VMEM((KEYS, HD), BF16),
            pltpu.VMEM((KEYS, HD), BF16),
            pltpu.VMEM((HD, KEYS), BF16),
            pltpu.VMEM((rows, HD), BF16),
            pltpu.VMEM((rows, HD), BF16),
            pltpu.VMEM((KEYS, HD), F32),
            pltpu.VMEM((KEYS, HD), F32),
            pltpu.VMEM((QB, HD, ROWS), F32),
            pltpu.VMEM((QB, ROWS), F32),
            pltpu.VMEM((QB, ROWS), F32),
        ],
        5 * rows * KEYS * HD,
    )(meta, *args)


def on_device(query_states, key_states, value_states, output_grad, positions):
    ids = (positions // SPAN).astype(BF16)
    kv, qg = pack_call(positions, query_states, key_states, value_states, output_grad)
    qa = send(qg, along_y(1))
    qb = send(qg, along_y(-1))
    pair = jnp.concatenate([kv, send(kv, to_core)], axis=0)
    third = send(pair, along_z(3))
    first = send(pair, along_z(1))
    qa, qb, first, third = lax.optimization_barrier((qa, qb, first, third))
    lower = lax.axis_index("outer") % NC == 0
    qc = send(jnp.where(lower, qa, qb), along_y_by_core)
    kb = send(jnp.concatenate([first, third[:SHARD]], axis=0), along_z(1))
    ka = jnp.concatenate([first, third], axis=0)
    xa = send(ka, to_core)
    kb, qc = lax.optimization_barrier((kb, qc))
    xb = send(kb, to_core)

    def ids_of(x):
        return x.reshape(-1, SHARD, 2 * HD)[:, TOK, 0:HD:SPAN].reshape(-1)

    kid = jnp.concatenate([ids_of(x) for x in (pair, ka, kb, xa, xb)]).astype(jnp.int32)
    qid = jnp.concatenate([ids[::SPAN]] + [x[TOK, 0:HD:SPAN] for x in (qa, qb, qc)]).astype(jnp.int32)
    rank = jnp.sum((kid[None, :] < kid[:, None]).astype(jnp.int32), axis=1)
    slots = jnp.arange(KB, dtype=jnp.int32)
    in_order = jnp.sum(jnp.where(rank[None, :] == slots[:, None], kid[None, :], 0), axis=1)
    below = jnp.sum((kid[None, :] < qid[:, None]).astype(jnp.int32), axis=1)
    upto = jnp.sum((kid[None, :] <= qid[:, None]).astype(jnp.int32), axis=1)
    whole = below // PER
    left = upto - whole * PER
    halves = ((left > 0) & (left <= PER // 2)).astype(jnp.int32)
    fulls = (left > PER // 2).astype(jnp.int32)
    meta = jnp.concatenate([rank, in_order, whole, halves, fulls, qid])

    args = (pair, ka, kb, xa, xb, query_states, output_grad, qa, qb, qc)
    st = fwd_call(meta, *args)
    stats = (st, send(st, along_y(1)), send(st, along_y(-1)), send(st, along_y(2)))
    dq, here, away = bwd_call(meta, *args, *stats)

    terms = [dq[0], send(dq[3], along_y(2)), send(dq[1], along_y(-1)), send(dq[2], along_y(1))]
    query_grad = sum(t.astype(F32) for t in terms).astype(BF16)
    both = here.astype(F32) + send(away, to_core).astype(F32)
    out = both[TOK:].astype(BF16)
    back = [
        send(out[2 * TOK:4 * TOK], along_z(-3)),
        send(out[4 * TOK:6 * TOK], along_z(-2)),
        send(out[:2 * TOK], along_z(-1)),
    ]
    back_far = send(out[6 * TOK:], along_z(-4))
    found = sum(t.astype(F32) for t in back)
    cross = send(found[TOK:].astype(BF16), to_core)
    pair_grad = both[:TOK] + back_far.astype(F32) + found[:TOK] + cross.astype(F32)
    return (
        query_grad,
        pair_grad[:, :HD].astype(BF16),
        pair_grad[:, HD:].astype(BF16),
    )


def solution(mesh):
    in_specs = (
        P(("inner", "outer"), "heads"),
        P(("inner", "outer"), "heads"),
        P(("inner", "outer"), "heads"),
        P(("inner", "outer"), "heads"),
        P(("inner", "outer")),
    )
    out_specs = (
        P(("inner", "outer"), "heads"),
        P(("inner", "outer"), "heads"),
        P(("inner", "outer"), "heads"),
    )
    return jax.shard_map(
        on_device, mesh=mesh, in_specs=in_specs, out_specs=out_specs, check_vma=False
    )
```
